256 devices in a mesh: lat: 32 (over z, x_hi, core), lon: 8 (over x_lo, y).
Axes of the slice: x: 4 (x_hi: 2, x_lo: 2; x = x_hi * 2 + x_lo), y: 4, z: 8, core: 2. Of those that a mesh axis runs over, the one named last changes fastest.
Arguments:
- kept_modes: bfloat16 [64, 90, 2, 768], P('lat', None, None, 'lon'), may hold values from -6 to 6
- decoder_weight: bfloat16 [768, 1280], replicated, may hold values from -0.21875 to 0.21875
- conv_in_weight: bfloat16 [3, 3, 20, 256], replicated, may hold values from -0.4375 to 0.4375
- conv_mid_weight: bfloat16 [3, 3, 256, 256], replicated, may hold values from -0.125 to 0.125
- conv_out_weight: bfloat16 [3, 3, 256, 1], replicated, may hold values from -0.125 to 0.125
Outputs:
- precipitation: float32 [512, 1440], P('lat', 'lon')
The draws below stay inside these ranges and needn't reach their ends.
All inputs are finite; a program needn't handle non-finite values.
Results may differ from the reference program's by a relative error of at most 0.025.
Values may be sent and summed in bfloat16 or wider, within the bound.
A program may use at most 128 MiB of HBM per device.

```python
import math
import jax
import jax.numpy as jnp
from jax import lax

D = 768
OUT = 20
CH = 256
LON_TOK = 180
MODES = 90
PATCH = 8
LAT_TOK = 64


def block_levels(rng, extent, shards, least, largest):
    def one(axis_at, blocks):
        steps = jax.random.uniform(jax.random.fold_in(jax.random.fold_in(rng, 6), axis_at), (blocks,), jnp.float32, least / len(shards), largest / len(shards))
        return jnp.repeat(jnp.exp(steps), extent[axis_at] // blocks).reshape((-1,) + (1,) * (len(extent) - axis_at - 1))

    loudness = one(*shards[0])
    for cut in shards[1:]:
        loudness = loudness * one(*cut)
    return loudness


def gaussian(own_key, shape, scale, reach, pieces=(), kind=jnp.bfloat16):
    gain = block_levels(own_key, shape, pieces, -0.22, 0.18) if pieces else 1.0
    array = jax.random.normal(own_key, shape, jnp.float32) * scale * gain
    return jnp.minimum(jnp.maximum(array, -reach), reach).astype(kind)


def setup_inputs(seed: int = 0) -> dict:
    splits = jax.random.split(jax.random.key(seed), 6)
    return {
        "kept_modes": gaussian(splits[0], (LAT_TOK, MODES, 2, D), 1.0, 6.0, ((0, 32), (3, 8))),
        "decoder_weight": gaussian(splits[1], (D, PATCH * PATCH * OUT), D ** -0.5, 0.21875),
        "conv_in_weight": gaussian(splits[2], (3, 3, OUT, CH), (9 * OUT) ** -0.5, 0.4375),
        "conv_mid_weight": gaussian(splits[3], (3, 3, CH, CH), (9 * CH) ** -0.5, 0.125),
        "conv_out_weight": gaussian(splits[4], (3, 3, CH, 1), (9 * CH) ** -0.5, 0.125),
    }


def spectral_table(token_ids, mode_count, length):
    mode_ids = jnp.arange(mode_count, dtype=jnp.int32)
    turns = token_ids[:, None] * mode_ids[None, :] % length
    phase_angle = turns.astype(jnp.float32) * (2.0 * math.pi / length)
    scaling = jnp.where(mode_ids == 0, 1.0, 2.0).astype(jnp.float32) / math.sqrt(length)
    dft_table = jnp.stack([scaling * jnp.cos(phase_angle), -scaling * jnp.sin(phase_angle)], axis=2)
    return dft_table.reshape(token_ids.shape[0], 2 * mode_count)

def conv_valid(x, weight):
    result = lax.conv_general_dilated(x.astype(jnp.float32)[None], weight.astype(jnp.float32), (1, 1), 'VALID', dimension_numbers=('NHWC', 'HWIO', 'NHWC'), precision=lax.Precision.HIGHEST)
    return result[0]

def row_mask(h, first_row, pixel_rows):
    global_rows = first_row + jnp.arange(h.shape[0], dtype=jnp.int32)
    inside = (global_rows >= 0) & (global_rows < pixel_rows)
    return jnp.where(inside[:, None, None], h, jnp.zeros_like(h))

def reference(kept_modes, decoder_weight, conv_in_weight, conv_mid_weight, conv_out_weight):
    token_rows = kept_modes.shape[0]
    mode_count = kept_modes.shape[1]
    out_count = decoder_weight.shape[1] // (PATCH * PATCH)
    pixel_rows = token_rows * PATCH
    pixel_cols = LON_TOK * PATCH
    dft_table = spectral_table(jnp.arange(LON_TOK, dtype=jnp.int32), mode_count, LON_TOK)
    flat = kept_modes.astype(jnp.float32).reshape(token_rows, 2 * mode_count, D)
    spectral_field = jnp.einsum('jq,tqc->tjc', dft_table, flat, precision=lax.Precision.HIGHEST).astype(jnp.bfloat16)
    decoded = jnp.dot(spectral_field.reshape(token_rows * LON_TOK, D), decoder_weight, preferred_element_type=jnp.float32).astype(jnp.bfloat16)
    decoded = decoded.reshape(token_rows, LON_TOK, PATCH, PATCH, out_count)
    pixels = jnp.transpose(decoded, (0, 2, 1, 3, 4)).reshape(pixel_rows, pixel_cols, out_count)
    padded = jnp.pad(pixels, ((3, 3), (0, 0), (0, 0)))

    def one_row(token_row):
        base_row = token_row * PATCH
        band = lax.dynamic_slice_in_dim(padded, base_row, PATCH + 6, 0)
        band = jnp.concatenate([band[:, -3:], band, band[:, :3]], axis=1)
        first = jnp.maximum(conv_valid(band, conv_in_weight), 0.0)
        first = row_mask(first, base_row - 2, pixel_rows).astype(jnp.bfloat16)
        second = jnp.maximum(conv_valid(first, conv_mid_weight), 0.0)
        second = row_mask(second, base_row - 1, pixel_rows).astype(jnp.bfloat16)
        return conv_valid(second, conv_out_weight)[:, :, 0]
    stacked = lax.map(one_row, jnp.arange(token_rows, dtype=jnp.int32))
    return stacked.reshape(pixel_rows, pixel_cols)
```

```python
import math

import jax
import jax.numpy as jnp
import numpy as np
from jax import lax
from jax.experimental import pallas as pl
from jax.experimental.pallas import tpu as pltpu
from jax.sharding import PartitionSpec as P

MESH = pl.DeviceIdType.MESH
BF16 = jnp.bfloat16
F32 = jnp.float32

LON_TOK = 180
PATCH = 8
NLON = 8
COLS = 180
ROWS = 16
OUT = 20
CH = 256
TQ = 3
CG = 8
TOK = TQ * CG
RG = 2
RJ = 9
T = TQ * PATCH
SUB = RG * CG
FIRST_J = RJ + 2
PIX_J = RJ + 4
WIN = (T + 2) // 2
PITCH = (T + 2) * SUB
ROWL = PATCH * OUT


def first_token(sector):
    return (COLS * sector - 3) // PATCH


def dft_table(mode_count):
    ids = []
    for d in range(NLON):
        for tq in range(TQ):
            for cg in range(CG):
                ids.append((first_token(d) + cg * TQ + tq) % LON_TOK)
    modes = np.arange(mode_count)
    angle = (np.array(ids)[:, None] * modes[None, :] % LON_TOK) * (2.0 * math.pi / LON_TOK)
    scale = np.where(modes == 0, 1.0, 2.0) / math.sqrt(LON_TOK)
    table = np.stack([scale * np.cos(angle), -scale * np.sin(angle)], axis=2)
    table = table.reshape(len(ids), 2 * mode_count).astype(np.float32)
    high = table.astype(BF16)
    low = (table - high.astype(np.float32)).astype(BF16)
    return np.concatenate([high, low], axis=0)


def order_table():
    table = np.zeros((2, 3 * T * SUB, RG * CH), np.float32)
    for parity in range(2):
        offset = COLS * parity - PATCH * first_token(parity)
        for b in range(3):
            for q in range(COLS):
                col = q + offset - 1 + b
                cg, t = divmod(col, T)
                for rg in range(RG):
                    table[parity, b * T * SUB + t * SUB + rg * CG + cg, rg * CH + q] = 1.0
    return table.astype(BF16)


def exchange_kernel(
    modes_ref, table_ref, order_ref, dec_ref, in_ref, mid_ref, out_ref,
    field, dec_v, in_v, mid_v, out_v, order_v,
    modes_s, table_s, send, in_s, out_s, out_f,
    local_sem, dec_sem, send_sem, recv_sem,
):
    lat, lon = lax.axis_index("lat"), lax.axis_index("lon")
    nlat = lax.axis_size("lat")
    up, down = lax.rem(lat + nlat - 1, nlat), lax.rem(lat + 1, nlat)
    chans = modes_s.shape[3]
    mode_count = modes_s.shape[1]

    early = [
        pltpu.make_async_copy(modes_ref, modes_s, local_sem.at[0]),
        pltpu.make_async_copy(table_ref, table_s, local_sem.at[1]),
    ]
    late = [
        pltpu.make_async_copy(in_ref, in_s, local_sem.at[2]),
        pltpu.make_async_copy(out_ref, out_s, local_sem.at[3]),
    ]
    last = [
        pltpu.make_async_copy(
            dec_ref.at[k * chans : (k + 1) * chans], dec_v.at[k, 0:chans], dec_sem.at[k]
        )
        for k in range(NLON)
    ] + [
        pltpu.make_async_copy(mid_ref, mid_v, local_sem.at[4]),
        pltpu.make_async_copy(order_ref.at[lax.rem(lon, 2)], order_v, local_sem.at[5]),
    ]
    for copy in early:
        copy.start()
    barrier = pltpu.get_barrier_semaphore()
    for step in range(NLON):
        there = lax.rem(lon + step, NLON)
        for row in (up, down) if step == 0 else (up, down, lat):
            pl.semaphore_signal(
                barrier, inc=1, device_id={"lat": row, "lon": there}, device_id_type=MESH
            )
    for copy in late + last:
        copy.start()
    send[...] = jnp.zeros_like(send)
    for copy in early:
        copy.wait()
    for row in range(2):
        values = modes_s[row].reshape(2 * mode_count, chans)
        wide = jnp.dot(table_s[...], values, preferred_element_type=F32)
        half = wide.shape[0] // 2
        whole = (wide[:half] + wide[half:]).astype(BF16)
        send[:, row, :, 0:chans] = whole.reshape(NLON, TOK, chans)
    field[lon, 1:3] = send[lon]
    pl.semaphore_wait(barrier, 3 * NLON - 1)
    sends, receives = [], []
    for step in range(NLON):
        there = lax.rem(lon + step, NLON)
        origin = lax.rem(lon + NLON - step, NLON)
        for way, (row, source, target) in enumerate(
            ((up, 0, 3), (down, 1, 0), (lat, None, None))
        ):
            if way == 2 and step == 0:
                continue
            copy = pltpu.make_async_remote_copy(
                src_ref=send.at[there] if way == 2 else send.at[there, source],
                dst_ref=field.at[lon, 1:3] if way == 2 else field.at[lon, target],
                send_sem=send_sem.at[way, step],
                recv_sem=recv_sem.at[way, step],
                device_id={"lat": row, "lon": there},
                device_id_type=MESH,
            )
            copy.start()
            sends.append(copy)
            receives.append(
                pltpu.make_async_remote_copy(
                    src_ref=send.at[there] if way == 2 else send.at[there, source],
                    dst_ref=field.at[origin, 1:3] if way == 2 else field.at[origin, target],
                    send_sem=send_sem.at[way, step],
                    recv_sem=recv_sem.at[way, step],
                    device_id={"lat": row, "lon": there},
                    device_id_type=MESH,
                )
            )
    for copy in late:
        copy.wait()
    dec_v[:, chans:, :] = jnp.zeros((NLON, dec_v.shape[1] - chans, dec_v.shape[2]), BF16)
    for turn in range(3):
        for phase in range(2):
            rows = []
            for place in range(3):
                a = (place - turn) % 3
                if phase:
                    rows.append(jnp.zeros((OUT, CH), BF16))
                rows += [in_s[a, b] for b in range(3)]
                if not phase:
                    rows.append(jnp.zeros((OUT, CH), BF16))
            rows.append(jnp.zeros((16, CH), BF16))
            in_v[turn, :, phase * CH : (phase + 1) * CH] = jnp.concatenate(rows, axis=0)
    out_f[...] = jnp.zeros_like(out_f)
    for a in range(3):
        for b in range(3):
            out_f[b * 8 + a : b * 8 + a + 1, :] = out_s[a, b : b + 1, :].astype(F32)
    out_v[...] = out_f[...].astype(BF16)
    for copy in last:
        copy.wait()
    for copy in receives:
        copy.wait_recv()
    for copy in sends:
        copy.wait_send()


def head_kernel(
    field, dec_v, in_v, mid_v, out_v, order_v, result, tokens, pieces, first, taps, sums
):
    lat = lax.axis_index("lat")
    top, bottom = lat == 0, lat == lax.axis_size("lat") - 1
    flat = jnp.concatenate([field[k].reshape(4 * TOK, 128) for k in range(NLON)], axis=1)
    decoded = jnp.dot(
        flat, dec_v[...].reshape(NLON * 128, ROWL * PATCH), preferred_element_type=F32
    ).reshape(4, TQ, CG, ROWL * PATCH)
    tokens[0] = jnp.where(top, 0.0, decoded[0])
    tokens[1:3] = decoded[1:3]
    tokens[3] = jnp.where(bottom, 0.0, decoded[3])

    lane = lax.broadcasted_iota(jnp.int32, (CG, CH), 1)

    def placed(slot, tq, start, place):
        base = min(start // 128 * 128, ROWL * PATCH - CH)
        block = tokens[slot, tq, :, base : base + CH]
        shift = (place - (start - base)) % CH
        return pltpu.roll(block, shift, 1) if shift else block

    halves = {}
    for p in range(-3, 19):
        slot, pr, place = p // PATCH + 1, p % PATCH, p % 3 * 80
        for w in range(WIN - 1):
            tq, part = divmod(w, 4)
            if part:
                value = placed(slot, tq, pr * ROWL + (part - 1) * 40, place)
            else:
                before = placed(slot, (tq - 1) % TQ, pr * ROWL + 120, place)
                if tq == 0:
                    before = pltpu.roll(before, 1, 0)
                own = placed(slot, tq, pr * ROWL, place + 40)
                value = jnp.where(lane < place + 40, before, own)
            halves[p, w] = value
        before = placed(slot, TQ - 1, pr * ROWL + 120, place)
        after = pltpu.roll(placed(slot, 0, pr * ROWL, place + 40), CG - 1, 0)
        halves[p, WIN - 1] = jnp.where(lane < place + 40, before, after)
        if p >= 6:
            for w in range(WIN):
                pieces[p - 6, w] = jnp.concatenate(
                    [halves.pop((p - 9, w)), halves[p, w]], axis=0
                ).astype(BF16)

    lane2 = lax.broadcasted_iota(jnp.int32, (SUB, CH), 1)
    side = lax.broadcasted_iota(jnp.int32, (SUB, CH), 0) // CG
    for j in range(FIRST_J):
        ordered = [pieces[j + (c - j) % 3] for c in range(3)]
        window = jnp.where(
            lane2 < 80, ordered[0], jnp.where(lane2 < 160, ordered[1], ordered[2])
        ).reshape(WIN * SUB, CH)
        hidden = jnp.maximum(
            jnp.dot(window, in_v[j % 3], preferred_element_type=F32), 0.0
        ).reshape(WIN, SUB, 2 * CH)
        for phase in range(2):
            part = hidden[:, :, phase * CH : (phase + 1) * CH]
            if j < 2:
                part = jnp.where((side == 0) & top, 0.0, part)
            if j >= RJ:
                part = jnp.where((side == 1) & bottom, 0.0, part)
            first[j, :, phase * SUB : (phase + 1) * SUB, :] = part.astype(BF16)

    def mid_row(j, carry):
        blocks = []
        for a in range(3):
            for b in range(3):
                rows = first[j + a].reshape(PITCH, CH)
                blocks.append(rows[b * SUB : b * SUB + T * SUB])
        second = jnp.dot(
            jnp.concatenate(blocks, axis=1), mid_v[...], preferred_element_type=F32
        )
        second = jnp.maximum(second, 0.0).reshape(T, SUB, CH)
        outside = ((side == 0) & top & (j == 0)) | ((side == 1) & bottom & (j == RJ - 1))
        second = jnp.where(outside, 0.0, second).astype(BF16).reshape(T * SUB, CH)
        tap = lax.dot_general(
            out_v[...], second, (((1,), (1,)), ((), ())), preferred_element_type=F32
        )
        taps[j] = jnp.concatenate([tap[b * 8 : b * 8 + 8] for b in range(3)], axis=1)
        return carry

    lax.fori_loop(0, RJ, mid_row, 0)
    tap = taps[...].reshape(RJ * 8, 3 * T * SUB)
    high = tap.astype(BF16)
    low = (tap - high.astype(F32)).astype(BF16)
    moved = jnp.dot(
        jnp.concatenate([high, low], axis=0), order_v[...], preferred_element_type=F32
    )
    sums[...] = moved[: RJ * 8] + moved[RJ * 8 :]
    for p in range(ROWS):
        total = None
        for a in range(3):
            rg, j = divmod(p + a, RJ)
            term = sums[j * 8 + a : j * 8 + a + 1, rg * CH : rg * CH + COLS]
            total = term if total is None else total + term
        result[p : p + 1, :] = total


def per_device(kept_modes, decoder_weight, conv_in_weight, conv_mid_weight, conv_out_weight):
    mode_count, chans = kept_modes.shape[1], kept_modes.shape[3]
    table = dft_table(mode_count)
    order = order_table()
    vmem = pl.BlockSpec(memory_space=pltpu.VMEM)
    anywhere = pl.BlockSpec(memory_space=pl.ANY)
    dma = pltpu.SemaphoreType.DMA
    staged = pl.pallas_call(
        exchange_kernel,
        out_shape=(
            pltpu.VMEM((NLON, 4, TOK, 128), BF16),
            pltpu.VMEM((NLON, 128, ROWL * PATCH), BF16),
            pltpu.VMEM((3, CH, 2 * CH), BF16),
            pltpu.VMEM((9 * CH, CH), BF16),
            pltpu.VMEM((24, CH), BF16),
            pltpu.VMEM(order.shape[1:], BF16),
        ),
        in_specs=[anywhere] * 7,
        out_specs=(vmem,) * 6,
        scratch_shapes=[
            pltpu.VMEM(kept_modes.shape, BF16),
            pltpu.VMEM(table.shape, BF16),
            pltpu.VMEM((NLON, 2, TOK, 128), BF16),
            pltpu.VMEM(conv_in_weight.shape, BF16),
            pltpu.VMEM((3, 3, CH), BF16),
            pltpu.VMEM((24, CH), F32),
            dma((6,)),
            dma((NLON,)),
            dma((3, NLON)),
            dma((3, NLON)),
        ],
        compiler_params=pltpu.CompilerParams(
            collective_id=0, has_side_effects=True, vmem_limit_bytes=24 * 2**20
        ),
        name="exchange",
    )(
        kept_modes,
        jnp.asarray(table),
        jnp.asarray(order),
        decoder_weight,
        conv_in_weight,
        conv_mid_weight.reshape(9 * CH, CH),
        conv_out_weight.reshape(3, 3, CH),
    )
    staged = [pltpu.with_memory_space_constraint(x, pltpu.VMEM) for x in staged]
    return pl.pallas_call(
        head_kernel,
        out_shape=jax.ShapeDtypeStruct((ROWS, COLS), F32),
        in_specs=[vmem] * 6,
        out_specs=vmem,
        scratch_shapes=[
            pltpu.VMEM((4, TQ, CG, ROWL * PATCH), F32),
            pltpu.VMEM((PIX_J, WIN, SUB, CH), BF16),
            pltpu.VMEM((FIRST_J, WIN, 2 * SUB, CH), BF16),
            pltpu.VMEM((RJ, 8, 3 * T * SUB), F32),
            pltpu.VMEM((RJ * 8, RG * CH), F32),
        ],
        compiler_params=pltpu.CompilerParams(vmem_limit_bytes=32 * 2**20),
        name="head",
    )(*staged)


def solution(mesh):
    placed = (P("lat", None, None, "lon"), P(), P(), P(), P())
    return jax.shard_map(
        per_device, mesh=mesh, in_specs=placed, out_specs=P("lat", "lon"), check_vma=False
    )
```

```python
import math

import jax
import jax.numpy as jnp
import numpy as np
from jax import lax
from jax.experimental import pallas as pl
from jax.experimental.pallas import tpu as pltpu
from jax.sharding import PartitionSpec as P

MESH = pl.DeviceIdType.MESH
BF16 = jnp.bfloat16
F32 = jnp.float32

LON_TOK = 180
PATCH = 8
NLON = 8
COLS = 180
ROWS = 16
OUT = 20
CH = 256
TQ = 3
CG = 8
TOK = TQ * CG
RG = 2
RJ = 9
T = TQ * PATCH
SUB = RG * CG
FIRST_J = RJ + 2
PIX_J = RJ + 4
WIN = (T + 2) // 2
PITCH = (T + 2) * SUB
ROWL = PATCH * OUT


def first_token(sector):
    return (COLS * sector - 3) // PATCH


def dft_table(mode_count):
    ids = []
    for d in range(NLON):
        for tq in range(TQ):
            for cg in range(CG):
                ids.append((first_token(d) + cg * TQ + tq) % LON_TOK)
    modes = np.arange(mode_count)
    angle = (np.array(ids)[:, None] * modes[None, :] % LON_TOK) * (2.0 * math.pi / LON_TOK)
    scale = np.where(modes == 0, 1.0, 2.0) / math.sqrt(LON_TOK)
    table = np.stack([scale * np.cos(angle), -scale * np.sin(angle)], axis=2)
    table = table.reshape(len(ids), 2 * mode_count).astype(np.float32)
    high = table.astype(BF16)
    low = (table - high.astype(np.float32)).astype(BF16)
    return np.concatenate([high, low], axis=0)


def order_table():
    table = np.zeros((2, 3 * T * SUB, RG * CH), np.float32)
    for parity in range(2):
        offset = COLS * parity - PATCH * first_token(parity)
        for b in range(3):
            for q in range(COLS):
                col = q + offset - 1 + b
                cg, t = divmod(col, T)
                for rg in range(RG):
                    table[parity, b * T * SUB + t * SUB + rg * CG + cg, rg * CH + q] = 1.0
    return table.astype(BF16)


def exchange_kernel(
    modes_ref, table_ref, order_ref, dec_ref, in_ref, mid_ref, out_ref,
    field, dec_v, in_v, mid_v, out_v, order_v,
    modes_s, table_s, send, in_s, out_s, out_f,
    local_sem, dec_sem, send_sem, recv_sem,
):
    lat, lon = lax.axis_index("lat"), lax.axis_index("lon")
    nlat = lax.axis_size("lat")
    up, down = lax.rem(lat + nlat - 1, nlat), lax.rem(lat + 1, nlat)
    chans = modes_s.shape[3]
    mode_count = modes_s.shape[1]

    early = [
        pltpu.make_async_copy(modes_ref, modes_s, local_sem.at[0]),
        pltpu.make_async_copy(table_ref, table_s, local_sem.at[1]),
    ]
    late = [
        pltpu.make_async_copy(in_ref, in_s, local_sem.at[2]),
        pltpu.make_async_copy(out_ref, out_s, local_sem.at[3]),
    ]
    last = [
        pltpu.make_async_copy(
            dec_ref.at[k * chans : (k + 1) * chans], dec_v.at[k, 0:chans], dec_sem.at[k]
        )
        for k in range(NLON)
    ] + [
        pltpu.make_async_copy(mid_ref, mid_v, local_sem.at[4]),
        pltpu.make_async_copy(order_ref.at[lax.rem(lon, 2)], order_v, local_sem.at[5]),
    ]
    for copy in early:
        copy.start()
    barrier = pltpu.get_barrier_semaphore()
    for step in range(NLON):
        there = lax.rem(lon + step, NLON)
        for row in (up, down) if step == 0 else (up, down, lat):
            pl.semaphore_signal(
                barrier, inc=1, device_id={"lat": row, "lon": there}, device_id_type=MESH
            )
    for copy in late + last:
        copy.start()
    send[...] = jnp.zeros_like(send)
    for copy in early:
        copy.wait()
    for row in range(2):
        values = modes_s[row].reshape(2 * mode_count, chans)
        wide = jnp.dot(table_s[...], values, preferred_element_type=F32)
        half = wide.shape[0] // 2
        whole = (wide[:half] + wide[half:]).astype(BF16)
        send[:, row, :, 0:chans] = whole.reshape(NLON, TOK, chans)
    field[lon, 1:3] = send[lon]
    pl.semaphore_wait(barrier, 3 * NLON - 1)
    sends, receives = [], []
    for step in range(NLON):
        there = lax.rem(lon + step, NLON)
        origin = lax.rem(lon + NLON - step, NLON)
        for way, (row, source, target) in enumerate(
            ((up, 0, 3), (down, 1, 0), (lat, None, None))
        ):
            if way == 2 and step == 0:
                continue
            copy = pltpu.make_async_remote_copy(
                src_ref=send.at[there] if way == 2 else send.at[there, source],
                dst_ref=field.at[lon, 1:3] if way == 2 else field.at[lon, target],
                send_sem=send_sem.at[way, step],
                recv_sem=recv_sem.at[way, step],
                device_id={"lat": row, "lon": there},
                device_id_type=MESH,
            )
            copy.start()
            sends.append(copy)
            receives.append(
                pltpu.make_async_remote_copy(
                    src_ref=send.at[there] if way == 2 else send.at[there, source],
                    dst_ref=field.at[origin, 1:3] if way == 2 else field.at[origin, target],
                    send_sem=send_sem.at[way, step],
                    recv_sem=recv_sem.at[way, step],
                    device_id={"lat": row, "lon": there},
                    device_id_type=MESH,
                )
            )
    for copy in late:
        copy.wait()
    dec_v[:, chans:, :] = jnp.zeros((NLON, dec_v.shape[1] - chans, dec_v.shape[2]), BF16)
    for turn in range(3):
        for phase in range(2):
            rows = []
            for place in range(3):
                a = (place - turn) % 3
                if phase:
                    rows.append(jnp.zeros((OUT, CH), BF16))
                rows += [in_s[a, b] for b in range(3)]
                if not phase:
                    rows.append(jnp.zeros((OUT, CH), BF16))
            rows.append(jnp.zeros((16, CH), BF16))
            in_v[turn, :, phase * CH : (phase + 1) * CH] = jnp.concatenate(rows, axis=0)
    out_f[...] = jnp.zeros_like(out_f)
    for a in range(3):
        for b in range(3):
            out_f[b * 8 + a : b * 8 + a + 1, :] = out_s[a, b : b + 1, :].astype(F32)
    out_v[...] = out_f[...].astype(BF16)
    for copy in last:
        copy.wait()
    for copy in receives:
        copy.wait_recv()
    for copy in sends:
        copy.wait_send()


def head_kernel(
    field, dec_v, in_v, mid_v, out_v, order_v, result, tokens, pieces, first, taps, sums
):
    lat = lax.axis_index("lat")
    top, bottom = lat == 0, lat == lax.axis_size("lat") - 1
    flat = jnp.concatenate([field[k].reshape(4 * TOK, 128) for k in range(NLON)], axis=1)
    decoded = jnp.dot(
        flat, dec_v[...].reshape(NLON * 128, ROWL * PATCH), preferred_element_type=F32
    ).reshape(4, TQ, CG, ROWL * PATCH)
    tokens[0] = jnp.where(top, 0.0, decoded[0])
    tokens[1:3] = decoded[1:3]
    tokens[3] = jnp.where(bottom, 0.0, decoded[3])

    lane = lax.broadcasted_iota(jnp.int32, (CG, CH), 1)

    def placed(slot, tq, start, place):
        base = min(start // 128 * 128, ROWL * PATCH - CH)
        block = tokens[slot, tq, :, base : base + CH]
        shift = (place - (start - base)) % CH
        return pltpu.roll(block, shift, 1) if shift else block

    halves = {}
    for p in range(-3, 19):
        slot, pr, place = p // PATCH + 1, p % PATCH, p % 3 * 80
        for w in range(WIN - 1):
            tq, part = divmod(w, 4)
            if part:
                value = placed(slot, tq, pr * ROWL + (part - 1) * 40, place)
            else:
                before = placed(slot, (tq - 1) % TQ, pr * ROWL + 120, place)
                if tq == 0:
                    before = pltpu.roll(before, 1, 0)
                own = placed(slot, tq, pr * ROWL, place + 40)
                value = jnp.where(lane < place + 40, before, own)
            halves[p, w] = value
        before = placed(slot, TQ - 1, pr * ROWL + 120, place)
        after = pltpu.roll(placed(slot, 0, pr * ROWL, place + 40), CG - 1, 0)
        halves[p, WIN - 1] = jnp.where(lane < place + 40, before, after)
        if p >= 6:
            for w in range(WIN):
                pieces[p - 6, w] = jnp.concatenate(
                    [halves.pop((p - 9, w)), halves[p, w]], axis=0
                ).astype(BF16)

    lane2 = lax.broadcasted_iota(jnp.int32, (SUB, CH), 1)
    side = lax.broadcasted_iota(jnp.int32, (SUB, CH), 0) // CG
    for j in range(FIRST_J):
        ordered = [pieces[j + (c - j) % 3] for c in range(3)]
        window = jnp.where(
            lane2 < 80, ordered[0], jnp.where(lane2 < 160, ordered[1], ordered[2])
        ).reshape(WIN * SUB, CH)
        hidden = jnp.maximum(
            jnp.dot(window, in_v[j % 3], preferred_element_type=F32), 0.0
        ).reshape(WIN, SUB, 2 * CH)
        for phase in range(2):
            part = hidden[:, :, phase * CH : (phase + 1) * CH]
            if j < 2:
                part = jnp.where((side == 0) & top, 0.0, part)
            if j >= RJ:
                part = jnp.where((side == 1) & bottom, 0.0, part)
            first[j, :, phase * SUB : (phase + 1) * SUB, :] = part.astype(BF16)

    def mid_row(j, carry):
        blocks = []
        for a in range(3):
            for b in range(3):
                rows = first[j + a].reshape(PITCH, CH)
                blocks.append(rows[b * SUB : b * SUB + T * SUB])
        second = jnp.dot(
            jnp.concatenate(blocks, axis=1), mid_v[...], preferred_element_type=F32
        )
        second = jnp.maximum(second, 0.0).reshape(T, SUB, CH)
        outside = ((side == 0) & top & (j == 0)) | ((side == 1) & bottom & (j == RJ - 1))
        second = jnp.where(outside, 0.0, second).astype(BF16).reshape(T * SUB, CH)
        tap = lax.dot_general(
            out_v[...], second, (((1,), (1,)), ((), ())), preferred_element_type=F32
        )
        taps[j] = jnp.concatenate([tap[b * 8 : b * 8 + 8] for b in range(3)], axis=1)
        return carry

    lax.fori_loop(0, RJ, mid_row, 0)
    tap = taps[...].reshape(RJ * 8, 3 * T * SUB)
    high = tap.astype(BF16)
    low = (tap - high.astype(F32)).astype(BF16)
    moved = jnp.dot(
        jnp.concatenate([high, low], axis=0), order_v[...], preferred_element_type=F32
    )
    sums[...] = moved[: RJ * 8] + moved[RJ * 8 :]
    for p in range(ROWS):
        total = None
        for a in range(3):
            rg, j = divmod(p + a, RJ)
            term = sums[j * 8 + a : j * 8 + a + 1, rg * CH : rg * CH + COLS]
            total = term if total is None else total + term
        result[p : p + 1, :] = total


def per_device(kept_modes, decoder_weight, conv_in_weight, conv_mid_weight, conv_out_weight):
    mode_count, chans = kept_modes.shape[1], kept_modes.shape[3]
    table = dft_table(mode_count)
    order = order_table()
    vmem = pl.BlockSpec(memory_space=pltpu.VMEM)
    anywhere = pl.BlockSpec(memory_space=pltpu.HBM)
    dma = pltpu.SemaphoreType.DMA
    staged = pl.pallas_call(
        exchange_kernel,
        out_shape=(
            pltpu.VMEM((NLON, 4, TOK, 128), BF16),
            pltpu.VMEM((NLON, 128, ROWL * PATCH), BF16),
            pltpu.VMEM((3, CH, 2 * CH), BF16),
            pltpu.VMEM((9 * CH, CH), BF16),
            pltpu.VMEM((24, CH), BF16),
            pltpu.VMEM(order.shape[1:], BF16),
        ),
        in_specs=[anywhere] * 7,
        out_specs=(vmem,) * 6,
        scratch_shapes=[
            pltpu.VMEM(kept_modes.shape, BF16),
            pltpu.VMEM(table.shape, BF16),
            pltpu.VMEM((NLON, 2, TOK, 128), BF16),
            pltpu.VMEM(conv_in_weight.shape, BF16),
            pltpu.VMEM((3, 3, CH), BF16),
            pltpu.VMEM((24, CH), F32),
            dma((6,)),
            dma((NLON,)),
            dma((3, NLON)),
            dma((3, NLON)),
        ],
        compiler_params=pltpu.CompilerParams(
            collective_id=0, has_side_effects=True, vmem_limit_bytes=24 * 2**20
        ),
        name="exchange",
    )(
        *[
            pltpu.with_memory_space_constraint(x, pltpu.HBM)
            for x in (
                kept_modes,
                jnp.asarray(table),
                jnp.asarray(order),
                decoder_weight,
                conv_in_weight,
                conv_mid_weight.reshape(9 * CH, CH),
                conv_out_weight.reshape(3, 3, CH),
            )
        ]
    )
    staged = [pltpu.with_memory_space_constraint(x, pltpu.VMEM) for x in staged]
    return pl.pallas_call(
        head_kernel,
        out_shape=jax.ShapeDtypeStruct((ROWS, COLS), F32),
        in_specs=[vmem] * 6,
        out_specs=vmem,
        scratch_shapes=[
            pltpu.VMEM((4, TQ, CG, ROWL * PATCH), F32),
            pltpu.VMEM((PIX_J, WIN, SUB, CH), BF16),
            pltpu.VMEM((FIRST_J, WIN, 2 * SUB, CH), BF16),
            pltpu.VMEM((RJ, 8, 3 * T * SUB), F32),
            pltpu.VMEM((RJ * 8, RG * CH), F32),
        ],
        compiler_params=pltpu.CompilerParams(vmem_limit_bytes=32 * 2**20),
        name="head",
    )(*staged)


def solution(mesh):
    placed = (P("lat", None, None, "lon"), P(), P(), P(), P())
    return jax.shard_map(
        per_device, mesh=mesh, in_specs=placed, out_specs=P("lat", "lon"), check_vma=False
    )
```

```python
import math

import jax
import jax.numpy as jnp
import numpy as np
from jax import lax
from jax.experimental import pallas as pl
from jax.experimental.pallas import tpu as pltpu
from jax.sharding import PartitionSpec as P

MESH = pl.DeviceIdType.MESH
BF16 = jnp.bfloat16
F32 = jnp.float32

LON_TOK = 180
PATCH = 8
NLON = 8
COLS = 180
ROWS = 16
OUT = 20
CH = 256
TQ = 3
CG = 8
TOK = TQ * CG
RG = 2
RJ = 9
T = TQ * PATCH
SUB = RG * CG
FIRST_J = RJ + 2
PIX_J = RJ + 4
JB = 3
WIN = (T + 2) // 2
PAIRS = T // 2
STEP = PAIRS * SUB
ROWL = PATCH * OUT


def first_token(sector):
    return (COLS * sector - 3) // PATCH


def dft_table(mode_count):
    ids = []
    for d in range(NLON):
        for tq in range(TQ):
            for cg in range(CG):
                ids.append((first_token(d) + cg * TQ + tq) % LON_TOK)
    modes = np.arange(mode_count)
    angle = (np.array(ids)[:, None] * modes[None, :] % LON_TOK) * (2.0 * math.pi / LON_TOK)
    scale = np.where(modes == 0, 1.0, 2.0) / math.sqrt(LON_TOK)
    table = np.stack([scale * np.cos(angle), -scale * np.sin(angle)], axis=2)
    table = table.reshape(len(ids), 2 * mode_count).astype(np.float32)
    high = table.astype(BF16)
    low = (table - high.astype(np.float32)).astype(BF16)
    return np.concatenate([high, low], axis=0)


def order_table():
    table = np.zeros((2, 3 * T * SUB, RG * CH), np.float32)
    for parity in range(2):
        offset = COLS * parity - PATCH * first_token(parity)
        for b in range(3):
            for q in range(COLS):
                col = q + offset - 1 + b
                cg, t = divmod(col, T)
                pair, phase = divmod(t, 2)
                at = (b * 2 + phase) * STEP + pair * SUB + cg
                for rg in range(RG):
                    table[parity, at + rg * CG, rg * CH + q] = 1.0
    return table.astype(BF16)


def exchange_kernel(
    modes_ref, table_ref, order_ref, dec_ref, in_ref, mid_ref, out_ref,
    field, dec_v, in_v, mid_v, out_v, order_v,
    modes_s, table_s, send, in_s, mid_s, out_s, out_f,
    local_sem, dec_sem, mid_sem, send_sem, recv_sem,
):
    lat, lon = lax.axis_index("lat"), lax.axis_index("lon")
    nlat = lax.axis_size("lat")
    chans = modes_s.shape[3]
    mode_count = modes_s.shape[1]

    early = [
        pltpu.make_async_copy(modes_ref, modes_s, local_sem.at[0]),
        pltpu.make_async_copy(table_ref, table_s, local_sem.at[1]),
    ]
    late = [
        pltpu.make_async_copy(in_ref, in_s, local_sem.at[2]),
        pltpu.make_async_copy(out_ref, out_s, local_sem.at[3]),
    ]
    middle = [
        pltpu.make_async_copy(
            mid_ref.at[a * 3 + b],
            mid_s.at[a] if b == 1 else mid_v.at[3 * b // 2, a * CH : (a + 1) * CH],
            mid_sem.at[a, b],
        )
        for a in range(3)
        for b in range(3)
    ]
    last = [
        pltpu.make_async_copy(
            dec_ref.at[k * chans : (k + 1) * chans], dec_v.at[k, 0:chans], dec_sem.at[k]
        )
        for k in range(NLON)
    ] + [
        pltpu.make_async_copy(order_ref.at[lax.rem(lon, 2)], order_v, local_sem.at[4]),
    ]
    for copy in early:
        copy.start()
    barrier = pltpu.get_barrier_semaphore()

    def greet(row, steps):
        for step in steps:
            there = {"lat": row, "lon": lax.rem(lon + step, NLON)}
            pl.semaphore_signal(barrier, inc=1, device_id=there, device_id_type=MESH)

    has_up, has_down = lat > 0, lat < nlat - 1
    pl.when(has_up)(lambda: greet(lat - 1, range(NLON)))
    pl.when(has_down)(lambda: greet(lat + 1, range(NLON)))
    greet(lat, range(1, NLON))
    for copy in late + middle + last:
        copy.start()
    send[...] = jnp.zeros_like(send)
    for copy in early:
        copy.wait()
    for row in range(2):
        values = modes_s[row].reshape(2 * mode_count, chans)
        wide = jnp.dot(table_s[...], values, preferred_element_type=F32)
        half = wide.shape[0] // 2
        whole = (wide[:half] + wide[half:]).astype(BF16)
        send[:, row, :, 0:chans] = whole.reshape(NLON, TOK, chans)
    field[lon, 1:3] = send[lon]
    partners = NLON * (1 + has_up.astype(jnp.int32) + has_down.astype(jnp.int32)) - 1
    pl.semaphore_wait(barrier, partners)

    def transfer(way, step, mine):
        there = lax.rem(lon + step, NLON)
        owner = lon if mine else lax.rem(lon + NLON - step, NLON)
        source = (send.at[there, 0], send.at[there, 1], send.at[there])[way]
        target = (field.at[owner, 3], field.at[owner, 0], field.at[owner, 1:3])[way]
        return pltpu.make_async_remote_copy(
            src_ref=source,
            dst_ref=target,
            send_sem=send_sem.at[way, step],
            recv_sem=recv_sem.at[way, step],
            device_id={"lat": (lat - 1, lat + 1, lat)[way], "lon": there},
            device_id_type=MESH,
        )

    def each(way, action, mine):
        for step in range(1 if way == 2 else 0, NLON):
            action(transfer(way, step, mine))

    pl.when(has_up)(lambda: each(0, lambda copy: copy.start(), True))
    pl.when(has_down)(lambda: each(1, lambda copy: copy.start(), True))
    each(2, lambda copy: copy.start(), True)

    @pl.when(jnp.logical_not(has_up))
    def _():
        field[:, 0] = jnp.zeros((NLON, TOK, 128), BF16)

    @pl.when(jnp.logical_not(has_down))
    def _():
        field[:, 3] = jnp.zeros((NLON, TOK, 128), BF16)

    for copy in late:
        copy.wait()
    dec_v[:, chans:, :] = jnp.zeros((NLON, dec_v.shape[1] - chans, dec_v.shape[2]), BF16)
    for turn in range(3):
        for phase in range(2):
            rows = []
            for place in range(3):
                a = (place - turn) % 3
                if phase:
                    rows.append(jnp.zeros((OUT, CH), BF16))
                rows += [in_s[a, b] for b in range(3)]
                if not phase:
                    rows.append(jnp.zeros((OUT, CH), BF16))
            rows.append(jnp.zeros((16, CH), BF16))
            in_v[turn, :, phase * CH : (phase + 1) * CH] = jnp.concatenate(rows, axis=0)
    out_f[...] = jnp.zeros_like(out_f)
    for a in range(3):
        for b in range(3):
            out_f[b * 8 + a : b * 8 + a + 1, :] = out_s[a, b : b + 1, :].astype(F32)
    out_v[...] = out_f[...].astype(BF16)
    for copy in middle:
        copy.wait()
    for a in range(3):
        here = slice(a * CH, (a + 1) * CH)
        ends = mid_v[0, here].astype(F32) + mid_v[3, here].astype(F32)
        centre = mid_s[a].astype(F32)
        mid_v[1, here] = (0.5 * (ends + centre)).astype(BF16)
        mid_v[2, here] = (0.5 * (ends - centre)).astype(BF16)
    for copy in last:
        copy.wait()
    pl.when(has_up)(lambda: each(1, lambda copy: copy.wait_recv(), False))
    pl.when(has_down)(lambda: each(0, lambda copy: copy.wait_recv(), False))
    each(2, lambda copy: copy.wait_recv(), False)
    pl.when(has_up)(lambda: each(0, lambda copy: copy.wait_send(), True))
    pl.when(has_down)(lambda: each(1, lambda copy: copy.wait_send(), True))
    each(2, lambda copy: copy.wait_send(), True)


def head_kernel(
    field, dec_v, in_v, mid_v, out_v, order_v, result, tokens, pieces, first, taps, sums
):
    lat = lax.axis_index("lat")
    top, bottom = lat == 0, lat == lax.axis_size("lat") - 1
    flat = jnp.concatenate([field[k].reshape(4 * TOK, 128) for k in range(NLON)], axis=1)
    decoded = jnp.dot(
        flat, dec_v[...].reshape(NLON * 128, ROWL * PATCH), preferred_element_type=F32
    ).reshape(4, TQ, CG, ROWL * PATCH)
    tokens[...] = decoded

    lane = lax.broadcasted_iota(jnp.int32, (CG, CH), 1)

    def placed(slot, tq, start, place):
        base = min(start // 128 * 128, ROWL * PATCH - CH)
        block = tokens[slot, tq, :, base : base + CH]
        shift = (place - (start - base)) % CH
        return pltpu.roll(block, shift, 1) if shift else block

    halves = {}
    for p in range(-3, 19):
        slot, pr, place = p // PATCH + 1, p % PATCH, p % 3 * 80
        for w in range(WIN - 1):
            tq, part = divmod(w, 4)
            if part:
                value = placed(slot, tq, pr * ROWL + (part - 1) * 40, place)
            else:
                before = placed(slot, (tq - 1) % TQ, pr * ROWL + 120, place)
                if tq == 0:
                    before = pltpu.roll(before, 1, 0)
                own = placed(slot, tq, pr * ROWL, place + 40)
                value = jnp.where(lane < place + 40, before, own)
            halves[p, w] = value
        before = placed(slot, TQ - 1, pr * ROWL + 120, place)
        after = pltpu.roll(placed(slot, 0, pr * ROWL, place + 40), CG - 1, 0)
        halves[p, WIN - 1] = jnp.where(lane < place + 40, before, after)
        if p >= 6:
            for w in range(WIN):
                pieces[p - 6, w] = jnp.concatenate(
                    [halves.pop((p - 9, w)), halves[p, w]], axis=0
                ).astype(BF16)

    lane2 = lax.broadcasted_iota(jnp.int32, (SUB, CH), 1)
    side = lax.broadcasted_iota(jnp.int32, (SUB, CH), 0) // CG
    for j in range(FIRST_J):
        ordered = [pieces[j + (c - j) % 3] for c in range(3)]
        window = jnp.where(
            lane2 < 80, ordered[0], jnp.where(lane2 < 160, ordered[1], ordered[2])
        ).reshape(WIN * SUB, CH)
        hidden = jnp.maximum(
            jnp.dot(window, in_v[j % 3], preferred_element_type=F32), 0.0
        ).reshape(WIN, SUB, 2 * CH)
        even, odd = hidden[:, :, :CH], hidden[:, :, CH:]
        if j < 2:
            even = jnp.where((side == 0) & top, 0.0, even)
            odd = jnp.where((side == 0) & top, 0.0, odd)
        if j >= RJ:
            even = jnp.where((side == 1) & bottom, 0.0, even)
            odd = jnp.where((side == 1) & bottom, 0.0, odd)
        here = slice(j * STEP, (j + 1) * STEP)
        first[0, here] = (even[:-1] - even[1:]).reshape(STEP, CH).astype(BF16)
        first[1, here] = (odd[:-1] + even[1:]).reshape(STEP, CH).astype(BF16)
        first[2, here] = (even[1:] - odd[:-1]).reshape(STEP, CH).astype(BF16)
        first[3, here] = (odd[:-1] - odd[1:]).reshape(STEP, CH).astype(BF16)

    for part in range(RJ // JB):
        products = []
        for k in range(4):
            blocks = [
                first[k, (part * JB + a) * STEP : (part * JB + a + JB) * STEP] for a in range(3)
            ]
            products.append(
                jnp.dot(jnp.concatenate(blocks, axis=1), mid_v[k], preferred_element_type=F32)
            )
        pair = (
            products[0] + (products[1] + products[2]),
            (products[1] - products[2]) - products[3],
        )
        pair = [jnp.maximum(x, 0.0).reshape(JB, PAIRS, SUB, CH) for x in pair]
        for step in range(JB):
            j = part * JB + step
            seconds = []
            for x in pair:
                x = x[step]
                if j == 0:
                    x = jnp.where((side == 0) & top, 0.0, x)
                if j == RJ - 1:
                    x = jnp.where((side == 1) & bottom, 0.0, x)
                seconds.append(x.reshape(STEP, CH).astype(BF16))
            tap = lax.dot_general(
                out_v[...],
                jnp.concatenate(seconds, axis=0),
                (((1,), (1,)), ((), ())),
                preferred_element_type=F32,
            )
            taps[j] = jnp.concatenate([tap[b * 8 : b * 8 + 8] for b in range(3)], axis=1)

    tap = taps[...].reshape(RJ * 8, 3 * T * SUB)
    high = tap.astype(BF16)
    low = (tap - high.astype(F32)).astype(BF16)
    moved = jnp.dot(
        jnp.concatenate([high, low], axis=0), order_v[...], preferred_element_type=F32
    )
    sums[...] = moved[: RJ * 8] + moved[RJ * 8 :]
    for p in range(ROWS):
        total = None
        for a in range(3):
            rg, j = divmod(p + a, RJ)
            term = sums[j * 8 + a : j * 8 + a + 1, rg * CH : rg * CH + COLS]
            total = term if total is None else total + term
        result[p : p + 1, :] = total


def per_device(kept_modes, decoder_weight, conv_in_weight, conv_mid_weight, conv_out_weight):
    mode_count, chans = kept_modes.shape[1], kept_modes.shape[3]
    table = dft_table(mode_count)
    order = order_table()
    vmem = pl.BlockSpec(memory_space=pltpu.VMEM)
    anywhere = pl.BlockSpec(memory_space=pltpu.HBM)
    dma = pltpu.SemaphoreType.DMA
    staged = pl.pallas_call(
        exchange_kernel,
        out_shape=(
            pltpu.VMEM((NLON, 4, TOK, 128), BF16),
            pltpu.VMEM((NLON, 128, ROWL * PATCH), BF16),
            pltpu.VMEM((3, CH, 2 * CH), BF16),
            pltpu.VMEM((4, 3 * CH, CH), BF16),
            pltpu.VMEM((24, CH), BF16),
            pltpu.VMEM(order.shape[1:], BF16),
        ),
        in_specs=[anywhere] * 7,
        out_specs=(vmem,) * 6,
        scratch_shapes=[
            pltpu.VMEM(kept_modes.shape, BF16),
            pltpu.VMEM(table.shape, BF16),
            pltpu.VMEM((NLON, 2, TOK, 128), BF16),
            pltpu.VMEM(conv_in_weight.shape, BF16),
            pltpu.VMEM((3, CH, CH), BF16),
            pltpu.VMEM((3, 3, CH), BF16),
            pltpu.VMEM((24, CH), F32),
            dma((5,)),
            dma((NLON,)),
            dma((3, 3)),
            dma((3, NLON)),
            dma((3, NLON)),
        ],
        compiler_params=pltpu.CompilerParams(
            has_side_effects=True, collective_id=0, vmem_limit_bytes=24 * 2**20
        ),
        name="exchange",
    )(
        *[
            pltpu.with_memory_space_constraint(x, pltpu.HBM)
            for x in (
                kept_modes,
                jnp.asarray(table),
                jnp.asarray(order),
                decoder_weight,
                conv_in_weight,
                conv_mid_weight.reshape(9, CH, CH),
                conv_out_weight.reshape(3, 3, CH),
            )
        ]
    )
    staged = [pltpu.with_memory_space_constraint(x, pltpu.VMEM) for x in staged]
    return pl.pallas_call(
        head_kernel,
        out_shape=jax.ShapeDtypeStruct((ROWS, COLS), F32),
        in_specs=[vmem] * 6,
        out_specs=vmem,
        scratch_shapes=[
            pltpu.VMEM((4, TQ, CG, ROWL * PATCH), F32),
            pltpu.VMEM((PIX_J, WIN, SUB, CH), BF16),
            pltpu.VMEM((4, FIRST_J * STEP, CH), BF16),
            pltpu.VMEM((RJ, 8, 3 * T * SUB), F32),
            pltpu.VMEM((RJ * 8, RG * CH), F32),
        ],
        compiler_params=pltpu.CompilerParams(vmem_limit_bytes=32 * 2**20),
        name="head",
    )(*staged)


def solution(mesh):
    placed = (P("lat", None, None, "lon"), P(), P(), P(), P())
    return jax.shard_map(
        per_device, mesh=mesh, in_specs=placed, out_specs=P("lat", "lon"), check_vma=False
    )
```

```python
import math

import jax
import jax.numpy as jnp
import numpy as np
from jax import lax
from jax.experimental import pallas as pl
from jax.experimental.pallas import tpu as pltpu
from jax.sharding import PartitionSpec as P

MESH = pl.DeviceIdType.MESH
BF16 = jnp.bfloat16
F32 = jnp.float32

LON_TOK = 180
PATCH = 8
NLON = 8
COLS = 180
ROWS = 16
OUT = 20
FAR_FIRST = (2, 6, 1, 7, 3, 5, 4, 0)
CH = 256
TQ = 3
CG = 8
TOK = TQ * CG
RG = 2
RJ = 9
T = TQ * PATCH
SUB = RG * CG
FIRST_J = RJ + 2
PIX_J = RJ + 4
WIN = (T + 2) // 2
PAIRS = T // 2
STEP = PAIRS * SUB
ROWL = PATCH * OUT


def first_token(sector):
    return (COLS * sector - 3) // PATCH


def dft_table(mode_count):
    ids = []
    for d in range(NLON):
        for tq in range(TQ):
            for cg in range(CG):
                ids.append((first_token(d) + cg * TQ + tq) % LON_TOK)
    modes = np.arange(mode_count)
    angle = (np.array(ids)[:, None] * modes[None, :] % LON_TOK) * (2.0 * math.pi / LON_TOK)
    scale = np.where(modes == 0, 1.0, 2.0) / math.sqrt(LON_TOK)
    table = np.stack([scale * np.cos(angle), -scale * np.sin(angle)], axis=2)
    table = table.reshape(len(ids), 2 * mode_count).astype(np.float32)
    high = table.astype(BF16)
    low = (table - high.astype(np.float32)).astype(BF16)
    return np.concatenate([high, low], axis=0)


def order_table():
    table = np.zeros((2, 3 * T * SUB, RG * CH), np.float32)
    for parity in range(2):
        offset = COLS * parity - PATCH * first_token(parity)
        for b in range(3):
            for q in range(COLS):
                col = q + offset - 1 + b
                cg, t = divmod(col, T)
                pair, phase = divmod(t, 2)
                at = (b * 2 + phase) * STEP + pair * SUB + cg
                for rg in range(RG):
                    table[parity, at + rg * CG, rg * CH + q] = 1.0
    return table.astype(BF16)


def field_kernel(
    modes_ref, table_ref, order_ref, dec_ref, in_ref, mid_ref, out_ref,
    taps, order_v,
    field, dec_v, in_v, mid_v, out_v, tokens, pieces, first,
    modes_s, table_s, send, in_s, mid_s, out_s, out_f,
    local_sem, dec_sem, mid_sem, send_sem, recv_sem,
):
    lat, lon = lax.axis_index("lat"), lax.axis_index("lon")
    nlat = lax.axis_size("lat")
    chans = modes_s.shape[3]
    mode_count = modes_s.shape[1]

    early = [
        pltpu.make_async_copy(modes_ref, modes_s, local_sem.at[0]),
        pltpu.make_async_copy(table_ref, table_s, local_sem.at[1]),
    ]
    late = [
        pltpu.make_async_copy(in_ref, in_s, local_sem.at[2]),
        pltpu.make_async_copy(out_ref, out_s, local_sem.at[3]),
    ]
    middle = [
        pltpu.make_async_copy(
            mid_ref.at[a * 3 + b],
            mid_s.at[a] if b == 1 else mid_v.at[3 * b // 2, a * CH : (a + 1) * CH],
            mid_sem.at[a, b],
        )
        for a in range(3)
        for b in range(3)
    ]
    last = [
        pltpu.make_async_copy(
            dec_ref.at[k * chans : (k + 1) * chans], dec_v.at[k, 0:chans], dec_sem.at[k]
        )
        for k in range(NLON)
    ] + [
        pltpu.make_async_copy(order_ref.at[lax.rem(lon, 2)], order_v, local_sem.at[4]),
    ]
    for copy in early:
        copy.start()
    barrier = pltpu.get_barrier_semaphore()

    def greet(row, steps):
        for step in steps:
            there = {"lat": row, "lon": lax.rem(lon + step, NLON)}
            pl.semaphore_signal(barrier, inc=1, device_id=there, device_id_type=MESH)

    has_up, has_down = lat > 0, lat < nlat - 1
    even = lax.rem(lat, 2) == 0
    pl.when(even & has_up)(lambda: greet(lat - 1, FAR_FIRST))
    pl.when(jnp.logical_not(even) & has_down)(lambda: greet(lat + 1, FAR_FIRST))
    greet(lat, FAR_FIRST[:-1])
    pl.when(even)(lambda: greet(lat + 1, FAR_FIRST))
    pl.when(jnp.logical_not(even))(lambda: greet(lat - 1, FAR_FIRST))
    for copy in late + middle + last:
        copy.start()
    send[...] = jnp.zeros_like(send)
    for copy in early:
        copy.wait()
    for row in range(2):
        values = modes_s[row].reshape(2 * mode_count, chans)
        wide = jnp.dot(table_s[...], values, preferred_element_type=F32)
        half = wide.shape[0] // 2
        whole = (wide[:half] + wide[half:]).astype(BF16)
        send[:, row, :, 0:chans] = whole.reshape(NLON, TOK, chans)
    field[lon, 1:3] = send[lon]
    partners = NLON * (1 + has_up.astype(jnp.int32) + has_down.astype(jnp.int32)) - 1
    pl.semaphore_wait(barrier, partners)

    def transfer(way, step, mine):
        there = lax.rem(lon + step, NLON)
        owner = lon if mine else lax.rem(lon + NLON - step, NLON)
        source = (send.at[there, 0], send.at[there, 1], send.at[there])[way]
        target = (field.at[owner, 3], field.at[owner, 0], field.at[owner, 1:3])[way]
        return pltpu.make_async_remote_copy(
            src_ref=source,
            dst_ref=target,
            send_sem=send_sem.at[way, step],
            recv_sem=recv_sem.at[way, step],
            device_id={"lat": (lat - 1, lat + 1, lat)[way], "lon": there},
            device_id_type=MESH,
        )

    def each(way, action, mine):
        for step in FAR_FIRST[:-1] if way == 2 else FAR_FIRST:
            action(transfer(way, step, mine))

    def begin(copy):
        copy.start()

    each(2, begin, True)
    pl.when(even & has_up)(lambda: each(0, begin, True))
    pl.when(jnp.logical_not(even) & has_down)(lambda: each(1, begin, True))
    pl.when(even)(lambda: each(1, begin, True))
    pl.when(jnp.logical_not(even))(lambda: each(0, begin, True))

    @pl.when(jnp.logical_not(has_up))
    def _():
        field[:, 0] = jnp.zeros((NLON, TOK, 128), BF16)

    @pl.when(jnp.logical_not(has_down))
    def _():
        field[:, 3] = jnp.zeros((NLON, TOK, 128), BF16)

    for copy in late:
        copy.wait()
    dec_v[:, chans:, :] = jnp.zeros((NLON, dec_v.shape[1] - chans, dec_v.shape[2]), BF16)
    for turn in range(3):
        for phase in range(2):
            rows = []
            for place in range(3):
                a = (place - turn) % 3
                if phase:
                    rows.append(jnp.zeros((OUT, CH), BF16))
                rows += [in_s[a, b] for b in range(3)]
                if not phase:
                    rows.append(jnp.zeros((OUT, CH), BF16))
            rows.append(jnp.zeros((16, CH), BF16))
            in_v[turn, :, phase * CH : (phase + 1) * CH] = jnp.concatenate(rows, axis=0)
    out_f[...] = jnp.zeros_like(out_f)
    for a in range(3):
        for b in range(3):
            out_f[b * 8 + a : b * 8 + a + 1, :] = out_s[a, b : b + 1, :].astype(F32)
    out_v[...] = out_f[...].astype(BF16)
    for copy in middle:
        copy.wait()
    for a in range(3):
        here = slice(a * CH, (a + 1) * CH)
        ends = mid_v[0, here].astype(F32) + mid_v[3, here].astype(F32)
        centre = mid_s[a].astype(F32)
        mid_v[1, here] = (0.5 * (ends + centre)).astype(BF16)
        mid_v[2, here] = (0.5 * (ends - centre)).astype(BF16)
    for copy in last[:NLON]:
        copy.wait()
    each(2, lambda copy: copy.wait_recv(), False)

    top, bottom = jnp.logical_not(has_up), jnp.logical_not(has_down)
    weights = dec_v.reshape(NLON * 128, ROWL * PATCH)

    def decode(low, high, start, stop):
        count = high - low
        values = jnp.concatenate(
            [field[k, low:high].reshape(count * TOK, 128) for k in range(NLON)], axis=1
        )
        tokens[low:high, :, :, start:stop] = jnp.dot(
            values, weights[:, start:stop], preferred_element_type=F32
        ).reshape(count, TQ, CG, stop - start)

    lane = lax.broadcasted_iota(jnp.int32, (CG, CH), 1)

    def placed(slot, tq, start, place):
        base = min(start // 128 * 128, ROWL * PATCH - CH)
        block = tokens[slot, tq, :, base : base + CH]
        shift = (place - (start - base)) % CH
        return pltpu.roll(block, shift, 1) if shift else block

    def half(p, w):
        slot, pr, place = p // PATCH + 1, p % PATCH, p % 3 * 80
        tq, part = divmod(w, 4)
        if part:
            return placed(slot, tq, pr * ROWL + (part - 1) * 40, place)
        before = placed(slot, (tq - 1) % TQ, pr * ROWL + 120, place)
        own = placed(slot, tq % TQ, pr * ROWL, place + 40)
        if tq == 0:
            before = pltpu.roll(before, 1, 0)
        if tq == TQ:
            own = pltpu.roll(own, CG - 1, 0)
        return jnp.where(lane < place + 40, before, own)

    def spread(rows):
        for i in rows:
            for w in range(WIN):
                pieces[i, w] = jnp.concatenate(
                    [half(i - 3, w), half(i - 3 + RJ, w)], axis=0
                ).astype(BF16)

    lane2 = lax.broadcasted_iota(jnp.int32, (SUB, CH), 1)
    side = lax.broadcasted_iota(jnp.int32, (SUB, CH), 0) // CG

    def first_rows(rows):
        for j in rows:
            ordered = [pieces[j + (c - j) % 3] for c in range(3)]
            window = jnp.where(
                lane2 < 80, ordered[0], jnp.where(lane2 < 160, ordered[1], ordered[2])
            ).reshape(WIN * SUB, CH)
            hidden = jnp.maximum(
                jnp.dot(window, in_v[j % 3], preferred_element_type=F32), 0.0
            ).reshape(WIN, SUB, 2 * CH)
            left, right = hidden[:, :, :CH], hidden[:, :, CH:]
            if j < 2:
                left = jnp.where((side == 0) & top, 0.0, left)
                right = jnp.where((side == 0) & top, 0.0, right)
            if j >= RJ:
                left = jnp.where((side == 1) & bottom, 0.0, left)
                right = jnp.where((side == 1) & bottom, 0.0, right)
            here = slice(j * STEP, (j + 1) * STEP)
            first[0, here] = (left[:-1] - left[1:]).reshape(STEP, CH).astype(BF16)
            first[1, here] = (right[:-1] + left[1:]).reshape(STEP, CH).astype(BF16)
            first[2, here] = (left[1:] - right[:-1]).reshape(STEP, CH).astype(BF16)
            first[3, here] = (right[:-1] - right[1:]).reshape(STEP, CH).astype(BF16)

    def second_rows(low, count):
        products = []
        for k in range(4):
            blocks = [first[k, (low + a) * STEP : (low + a + count) * STEP] for a in range(3)]
            products.append(
                jnp.dot(jnp.concatenate(blocks, axis=1), mid_v[k], preferred_element_type=F32)
            )
        pair = (
            products[0] + (products[1] + products[2]),
            (products[1] - products[2]) - products[3],
        )
        pair = [jnp.maximum(x, 0.0).reshape(count, PAIRS, SUB, CH) for x in pair]
        for step in range(count):
            j = low + step
            seconds = []
            for x in pair:
                x = x[step]
                if j == 0:
                    x = jnp.where((side == 0) & top, 0.0, x)
                if j == RJ - 1:
                    x = jnp.where((side == 1) & bottom, 0.0, x)
                seconds.append(x.reshape(STEP, CH).astype(BF16))
            tap = lax.dot_general(
                out_v[...],
                jnp.concatenate(seconds, axis=0),
                (((1,), (1,)), ((), ())),
                preferred_element_type=F32,
            )
            taps[j] = jnp.concatenate([tap[b * 8 : b * 8 + 8] for b in range(3)], axis=1)

    decode(1, 3, 0, ROWL * PATCH)
    spread(range(3, 10))
    first_rows(range(3, 8))
    second_rows(3, 3)

    pl.when(has_up)(lambda: each(1, lambda copy: copy.wait_recv(), False))
    pl.when(has_down)(lambda: each(0, lambda copy: copy.wait_recv(), False))
    decode(0, 1, 768, ROWL * PATCH)
    decode(3, 4, 0, 512)
    spread((0, 1, 2, 10, 11, 12))
    first_rows((0, 1, 2, 8, 9, 10))
    second_rows(0, 3)
    second_rows(6, 3)

    for copy in last[NLON:]:
        copy.wait()
    pl.when(has_up)(lambda: each(0, lambda copy: copy.wait_send(), True))
    pl.when(has_down)(lambda: each(1, lambda copy: copy.wait_send(), True))
    each(2, lambda copy: copy.wait_send(), True)


def order_kernel(taps, order_v, result, sums):
    tap = taps[...].reshape(RJ * 8, 3 * T * SUB)
    high = tap.astype(BF16)
    low = (tap - high.astype(F32)).astype(BF16)
    moved = jnp.dot(
        jnp.concatenate([high, low], axis=0), order_v[...], preferred_element_type=F32
    )
    sums[...] = moved[: RJ * 8] + moved[RJ * 8 :]
    for p in range(ROWS):
        total = None
        for a in range(3):
            rg, j = divmod(p + a, RJ)
            term = sums[j * 8 + a : j * 8 + a + 1, rg * CH : rg * CH + COLS]
            total = term if total is None else total + term
        result[p : p + 1, :] = total


def per_device(kept_modes, decoder_weight, conv_in_weight, conv_mid_weight, conv_out_weight):
    mode_count, chans = kept_modes.shape[1], kept_modes.shape[3]
    table = dft_table(mode_count)
    order = order_table()
    vmem = pl.BlockSpec(memory_space=pltpu.VMEM)
    dma = pltpu.SemaphoreType.DMA
    staged = pl.pallas_call(
        field_kernel,
        out_shape=(
            pltpu.VMEM((RJ, 8, 3 * T * SUB), F32),
            pltpu.VMEM(order.shape[1:], BF16),
        ),
        in_specs=[pl.BlockSpec(memory_space=pltpu.HBM)] * 7,
        out_specs=(vmem,) * 2,
        scratch_shapes=[
            pltpu.VMEM((NLON, 4, TOK, 128), BF16),
            pltpu.VMEM((NLON, 128, ROWL * PATCH), BF16),
            pltpu.VMEM((3, CH, 2 * CH), BF16),
            pltpu.VMEM((4, 3 * CH, CH), BF16),
            pltpu.VMEM((24, CH), BF16),
            pltpu.VMEM((4, TQ, CG, ROWL * PATCH), F32),
            pltpu.VMEM((PIX_J, WIN, SUB, CH), BF16),
            pltpu.VMEM((4, FIRST_J * STEP, CH), BF16),
            pltpu.VMEM(kept_modes.shape, BF16),
            pltpu.VMEM(table.shape, BF16),
            pltpu.VMEM((NLON, 2, TOK, 128), BF16),
            pltpu.VMEM(conv_in_weight.shape, BF16),
            pltpu.VMEM((3, CH, CH), BF16),
            pltpu.VMEM((3, 3, CH), BF16),
            pltpu.VMEM((24, CH), F32),
            dma((5,)),
            dma((NLON,)),
            dma((3, 3)),
            dma((3, NLON)),
            dma((3, NLON)),
        ],
        compiler_params=pltpu.CompilerParams(
            collective_id=0, has_side_effects=True, vmem_limit_bytes=40 * 2**20
        ),
        name="field_to_taps",
    )(
        *[
            pltpu.with_memory_space_constraint(x, pltpu.HBM)
            for x in (
                kept_modes,
                jnp.asarray(table),
                jnp.asarray(order),
                decoder_weight,
                conv_in_weight,
                conv_mid_weight.reshape(9, CH, CH),
                conv_out_weight.reshape(3, 3, CH),
            )
        ]
    )
    staged = [pltpu.with_memory_space_constraint(x, pltpu.VMEM) for x in staged]
    return pl.pallas_call(
        order_kernel,
        out_shape=jax.ShapeDtypeStruct((ROWS, COLS), F32),
        in_specs=[vmem] * 2,
        out_specs=vmem,
        scratch_shapes=[pltpu.VMEM((RJ * 8, RG * CH), F32)],
        compiler_params=pltpu.CompilerParams(vmem_limit_bytes=16 * 2**20),
        name="order",
    )(*staged)


def solution(mesh):
    placed = (P("lat", None, None, "lon"), P(), P(), P(), P())
    return jax.shard_map(
        per_device, mesh=mesh, in_specs=placed, out_specs=P("lat", "lon"), check_vma=False
    )
```

```python
import math

import jax
import jax.numpy as jnp
import numpy as np
from jax import lax
from jax.experimental import pallas as pl
from jax.experimental.pallas import tpu as pltpu
from jax.sharding import PartitionSpec as P

MESH = pl.DeviceIdType.MESH
BF16 = jnp.bfloat16
F32 = jnp.float32

LON_TOK = 180
PATCH = 8
NLON = 8
COLS = 180
ROWS = 16
OUT = 20
FAR_FIRST = (2, 6, 1, 7, 3, 5, 4, 0)
CH = 256
TQ = 3
CG = 8
TOK = TQ * CG
SIDES = 2
T = TQ * PATCH // SIDES
SUB = SIDES * CG
WIN = (T + 2) // 2
PAIRS = T // 2
STEP = PAIRS * SUB
SECOND = ROWS + 2
FIRST = ROWS + 4
PIX = ROWS + 6
SECOND_ORDER = tuple(range(3, 15)) + (0, 1, 2, 15, 16, 17)
ROWL = PATCH * OUT
EDGE = 512


def first_token(sector):
    return (COLS * sector - 3) // PATCH


def dft_table(mode_count):
    ids = []
    for d in range(NLON):
        for tq in range(TQ):
            for cg in range(CG):
                ids.append((first_token(d) + cg * TQ + tq) % LON_TOK)
    modes = np.arange(mode_count)
    angle = (np.array(ids)[:, None] * modes[None, :] % LON_TOK) * (2.0 * math.pi / LON_TOK)
    scale = np.where(modes == 0, 1.0, 2.0) / math.sqrt(LON_TOK)
    table = np.stack([scale * np.cos(angle), -scale * np.sin(angle)], axis=2)
    table = table.reshape(len(ids), 2 * mode_count).astype(np.float32)
    high = table.astype(BF16)
    low = (table - high.astype(np.float32)).astype(BF16)
    return np.concatenate([high, low], axis=0)


def order_table():
    table = np.zeros((2, 3 * 4 * STEP, 2 * CH), np.float32)
    for parity in range(2):
        offset = COLS * parity - PATCH * first_token(parity)
        for b in range(3):
            for q in range(COLS):
                cg, rest = divmod(q + offset - 1 + b, T * SIDES)
                side, t = divmod(rest, T)
                pair, phase = divmod(t, 2)
                at = (b * 4 + phase) * STEP + pair * SUB + side * CG + cg
                for row in range(2):
                    table[parity, at + row * 2 * STEP, row * CH + q] = 1.0
    return table.astype(BF16)


def field_kernel(
    modes_ref, table_ref, order_ref, dec_ref, in_ref, mid_ref, out_ref,
    taps, order_v,
    field, edges, halo, dec_v, in_v, mid_v, out_v, tokens, pieces, first,
    modes_s, table_s, send, in_s, mid_s, out_s, out_f,
    local_sem, dec_sem, mid_sem, send_sem, recv_sem, ready,
):
    lat, lon = lax.axis_index("lat"), lax.axis_index("lon")
    nlat = lax.axis_size("lat")
    chans = modes_s.shape[3]
    mode_count = modes_s.shape[1]

    early = [
        pltpu.make_async_copy(modes_ref, modes_s, local_sem.at[0]),
        pltpu.make_async_copy(table_ref, table_s, local_sem.at[1]),
    ]
    late = [
        pltpu.make_async_copy(in_ref, in_s, local_sem.at[2]),
        pltpu.make_async_copy(out_ref, out_s, local_sem.at[3]),
    ]
    middle = [
        pltpu.make_async_copy(
            mid_ref.at[a * 3 + b],
            mid_s.at[a] if b == 1 else mid_v.at[3 * b // 2, a * CH : (a + 1) * CH],
            mid_sem.at[a, b],
        )
        for a in range(3)
        for b in range(3)
    ]
    last = [
        pltpu.make_async_copy(
            dec_ref.at[k * chans : (k + 1) * chans], dec_v.at[k, 0:chans], dec_sem.at[k]
        )
        for k in range(NLON)
    ] + [
        pltpu.make_async_copy(order_ref.at[lax.rem(lon, 2)], order_v, local_sem.at[4]),
    ]
    for copy in early:
        copy.start()
    barrier = pltpu.get_barrier_semaphore()

    odd = lax.rem(lat, 2)
    near = lat + 1 - 2 * odd
    far = lat - 1 + 2 * odd
    has_far = (far >= 0) & (far < nlat)

    greets, greeted = has_far & (odd == 1), has_far & (odd == 0)

    def greet(semaphore, row, column):
        there = {"lat": row, "lon": column}
        pl.semaphore_signal(semaphore, inc=1, device_id=there, device_id_type=MESH)

    pl.when(greets)(lambda: greet(barrier, far, lon))
    for step in FAR_FIRST[:-1]:
        greet(barrier, lat, lax.rem(lon + step, NLON))
    greet(barrier, near, lon)
    for copy in late + middle + last:
        copy.start()
    send[...] = jnp.zeros_like(send)
    for copy in early:
        copy.wait()
    for row in range(2):
        values = modes_s[row].reshape(2 * mode_count, chans)
        wide = jnp.dot(table_s[...], values, preferred_element_type=F32)
        half = wide.shape[0] // 2
        whole = (wide[:half] + wide[half:]).astype(BF16)
        send[:, row, :, 0:chans] = whole.reshape(NLON, TOK, chans)
    for row in range(2):
        field[row, lon] = send[lon, row]
    pl.semaphore_wait(barrier, NLON + greeted.astype(jnp.int32))
    pl.when(greeted)(lambda: greet(ready, far, lon))

    def across(step, mine):
        there = lax.rem(lon + step, NLON)
        owner = lon if mine else lax.rem(lon + NLON - step, NLON)
        return pltpu.make_async_remote_copy(
            src_ref=send.at[there],
            dst_ref=field.at[:, owner],
            send_sem=send_sem.at[step],
            recv_sem=recv_sem.at[step],
            device_id={"lat": lat, "lon": there},
            device_id_type=MESH,
        )

    def onward(way, row, source, target):
        return pltpu.make_async_remote_copy(
            src_ref=edges.at[source],
            dst_ref=halo.at[target],
            send_sem=send_sem.at[NLON + way],
            recv_sem=recv_sem.at[NLON + way],
            device_id={"lat": row, "lon": lon},
            device_id_type=MESH,
        )

    to_near, from_near = (onward(0, near, 1 - odd, slot) for slot in (odd, 1 - odd))
    to_far, from_far = (onward(1, far, odd, slot) for slot in (1 - odd, odd))

    for step in FAR_FIRST[:-1]:
        across(step, True).start()

    @pl.when(jnp.logical_not(has_far))
    def _():
        halo[odd] = jnp.zeros(halo.shape[1:], BF16)

    for copy in late:
        copy.wait()
    dec_v[:, chans:, :] = jnp.zeros((NLON, dec_v.shape[1] - chans, dec_v.shape[2]), BF16)
    for turn in range(3):
        for phase in range(2):
            rows = []
            for place in range(3):
                a = (place - turn) % 3
                if phase:
                    rows.append(jnp.zeros((OUT, CH), BF16))
                rows += [in_s[a, b] for b in range(3)]
                if not phase:
                    rows.append(jnp.zeros((OUT, CH), BF16))
            rows.append(jnp.zeros((16, CH), BF16))
            in_v[turn, :, phase * CH : (phase + 1) * CH] = jnp.concatenate(rows, axis=0)
    out_f[...] = jnp.zeros_like(out_f)
    for a in range(3):
        for b in range(3):
            out_f[b * 8 + a : b * 8 + a + 1, :] = out_s[a, b : b + 1, :].astype(F32)
    out_v[...] = out_f[...].astype(BF16)
    for copy in middle:
        copy.wait()
    for a in range(3):
        here = slice(a * CH, (a + 1) * CH)
        ends = mid_v[0, here].astype(F32) + mid_v[3, here].astype(F32)
        centre = mid_s[a].astype(F32)
        mid_v[1, here] = (0.5 * (ends + centre)).astype(BF16)
        mid_v[2, here] = (0.5 * (ends - centre)).astype(BF16)
    for copy in last[:NLON]:
        copy.wait()
    for step in FAR_FIRST[:-1]:
        across(step, False).wait_recv()
    top, bottom = lat == 0, lat == nlat - 1
    weights = dec_v[...].reshape(NLON * 128, ROWL * PATCH)

    values = jnp.concatenate([field[:, k].reshape(2 * TOK, 128) for k in range(NLON)], axis=1)
    pixels = jnp.dot(values, weights, preferred_element_type=F32)
    edges[0] = pixels[:TOK, :EDGE].astype(BF16)
    edges[1] = pixels[TOK:, -EDGE:].astype(BF16)

    @pl.when(has_far)
    def _():
        pl.when(greets)(lambda: pl.semaphore_wait(ready, 1))
        to_far.start()

    to_near.start()
    tokens[1:3] = pixels.reshape(2, TQ, CG, ROWL * PATCH)

    lane = lax.broadcasted_iota(jnp.int32, (CG, CH), 1)

    def placed(slot, tq, start, place):
        base = min(start // 128 * 128, ROWL * PATCH - CH)
        block = tokens[slot, tq, :, base : base + CH]
        shift = (place - (start - base)) % CH
        return pltpu.roll(block, shift, 1) if shift else block

    def half(p, w):
        slot, pr, place = p // PATCH + 1, p % PATCH, p % 3 * 80
        tq, part = divmod(w, 4)
        if part:
            return placed(slot, tq, pr * ROWL + (part - 1) * 40, place)
        before = placed(slot, (tq - 1) % TQ, pr * ROWL + 120, place)
        own = placed(slot, tq % TQ, pr * ROWL, place + 40)
        if tq == 0:
            before = pltpu.roll(before, 1, 0)
        if tq == TQ:
            own = pltpu.roll(own, CG - 1, 0)
        return jnp.where(lane < place + 40, before, own)

    def spread(rows):
        for i in rows:
            values = [half(i - 3, w) for w in range(SIDES * PAIRS + 1)]
            for w in range(WIN):
                pieces[i, w] = jnp.concatenate([values[w], values[w + PAIRS]], axis=0).astype(BF16)

    lane2 = lax.broadcasted_iota(jnp.int32, (SUB, CH), 1)

    def first_rows(rows):
        for turn in range(3):
            mine = [j for j in rows if j % 3 == turn]
            windows = []
            for j in mine:
                parts = [pieces[j + (c - j) % 3] for c in range(3)]
                window = jnp.where(lane2 < 80, parts[0], jnp.where(lane2 < 160, parts[1], parts[2]))
                windows.append(window.reshape(WIN * SUB, CH))
            hidden = jnp.maximum(
                jnp.dot(
                    jnp.concatenate(windows, axis=0), in_v[turn], preferred_element_type=F32
                ),
                0.0,
            ).reshape(len(mine), WIN, SUB, 2 * CH)
            for at, j in enumerate(mine):
                left, right = hidden[at, :, :, :CH], hidden[at, :, :, CH:]
                if j < 2 or j >= FIRST - 2:
                    outside = top if j < 2 else bottom
                    left = jnp.where(outside, 0.0, left)
                    right = jnp.where(outside, 0.0, right)
                here = slice(j * STEP, (j + 1) * STEP)
                first[0, here] = (left[:-1] - left[1:]).reshape(STEP, CH).astype(BF16)
                first[1, here] = (right[:-1] + left[1:]).reshape(STEP, CH).astype(BF16)
                first[2, here] = (left[1:] - right[:-1]).reshape(STEP, CH).astype(BF16)
                first[3, here] = (right[:-1] - right[1:]).reshape(STEP, CH).astype(BF16)

    def second_rows(low, count):
        products = []
        for k in range(4):
            blocks = [first[k, (low + a) * STEP : (low + a + count) * STEP] for a in range(3)]
            products.append(
                jnp.dot(jnp.concatenate(blocks, axis=1), mid_v[k], preferred_element_type=F32)
            )
        pair = (
            products[0] + (products[1] + products[2]),
            (products[1] - products[2]) - products[3],
        )
        pair = [jnp.maximum(x, 0.0).reshape(count, STEP, CH) for x in pair]
        rows = []
        for step in range(count):
            values = [x[step] for x in pair]
            if low + step == 0:
                values = [jnp.where(top, 0.0, x) for x in values]
            if low + step == SECOND - 1:
                values = [jnp.where(bottom, 0.0, x) for x in values]
            rows += [x.astype(BF16) for x in values]
        return rows

    def last_taps(rows, slot):
        for i in range(0, len(rows), 4):
            tap = lax.dot_general(
                out_v[...],
                jnp.concatenate(rows[i : i + 4], axis=0),
                (((1,), (1,)), ((), ())),
                preferred_element_type=F32,
            )
            taps[slot + i // 4] = jnp.concatenate([tap[b * 8 : b * 8 + 8] for b in range(3)], axis=1)

    spread(range(3, 19))
    first_rows(range(3, 17))
    last_taps(second_rows(3, 6), 0)
    last_taps(second_rows(9, 6), 3)

    from_near.wait_recv()
    pl.when(has_far)(lambda: from_far.wait_recv())
    tokens[0, :, :, -EDGE:] = halo[0].astype(F32).reshape(TQ, CG, EDGE)
    tokens[3, :, :, :EDGE] = halo[1].astype(F32).reshape(TQ, CG, EDGE)
    spread((0, 1, 2, 19, 20, 21))
    first_rows((0, 1, 2, 17, 18, 19))
    last_taps(second_rows(0, 3) + second_rows(15, 3), 6)

    for copy in last[NLON:]:
        copy.wait()
    for step in FAR_FIRST[:-1]:
        across(step, True).wait_send()
    to_near.wait_send()
    pl.when(has_far)(lambda: to_far.wait_send())


def order_kernel(taps, order_v, result, sums):
    count = taps.shape[0] * 8
    tap = taps[...].reshape(count, 3 * 4 * STEP)
    high = tap.astype(BF16)
    low = (tap - high.astype(F32)).astype(BF16)
    moved = jnp.dot(
        jnp.concatenate([high, low], axis=0), order_v[...], preferred_element_type=F32
    )
    sums[...] = moved[:count] + moved[count:]
    for p in range(ROWS):
        total = None
        for a in range(3):
            slot, half = divmod(SECOND_ORDER.index(p + a), 2)
            term = sums[slot * 8 + a : slot * 8 + a + 1, half * CH : half * CH + COLS]
            total = term if total is None else total + term
        result[p : p + 1, :] = total


def per_device(kept_modes, decoder_weight, conv_in_weight, conv_mid_weight, conv_out_weight):
    mode_count, chans = kept_modes.shape[1], kept_modes.shape[3]
    table = dft_table(mode_count)
    order = order_table()
    vmem = pl.BlockSpec(memory_space=pltpu.VMEM)
    dma = pltpu.SemaphoreType.DMA
    staged = pl.pallas_call(
        field_kernel,
        out_shape=(
            pltpu.VMEM((SECOND // 2, 8, 3 * 4 * STEP), F32),
            pltpu.VMEM(order.shape[1:], BF16),
        ),
        in_specs=[pl.BlockSpec(memory_space=pltpu.HBM)] * 7,
        out_specs=(vmem,) * 2,
        scratch_shapes=[
            pltpu.VMEM((2, NLON, TOK, 128), BF16),
            pltpu.VMEM((2, TOK, EDGE), BF16),
            pltpu.VMEM((2, TOK, EDGE), BF16),
            pltpu.VMEM((NLON, 128, ROWL * PATCH), BF16),
            pltpu.VMEM((3, CH, 2 * CH), BF16),
            pltpu.VMEM((4, 3 * CH, CH), BF16),
            pltpu.VMEM((24, CH), BF16),
            pltpu.VMEM((4, TQ, CG, ROWL * PATCH), F32),
            pltpu.VMEM((PIX, WIN, SUB, CH), BF16),
            pltpu.VMEM((4, FIRST * STEP, CH), BF16),
            pltpu.VMEM(kept_modes.shape, BF16),
            pltpu.VMEM(table.shape, BF16),
            pltpu.VMEM((NLON, 2, TOK, 128), BF16),
            pltpu.VMEM(conv_in_weight.shape, BF16),
            pltpu.VMEM((3, CH, CH), BF16),
            pltpu.VMEM((3, 3, CH), BF16),
            pltpu.VMEM((24, CH), F32),
            dma((5,)),
            dma((NLON,)),
            dma((3, 3)),
            dma((NLON + 2,)),
            dma((NLON + 2,)),
            pltpu.SemaphoreType.REGULAR,
        ],
        compiler_params=pltpu.CompilerParams(
            collective_id=0, has_side_effects=True, vmem_limit_bytes=40 * 2**20
        ),
        name="field_to_taps",
    )(
        *[
            pltpu.with_memory_space_constraint(x, pltpu.HBM)
            for x in (
                kept_modes,
                jnp.asarray(table),
                jnp.asarray(order),
                decoder_weight,
                conv_in_weight,
                conv_mid_weight.reshape(9, CH, CH),
                conv_out_weight.reshape(3, 3, CH),
            )
        ]
    )
    staged = [pltpu.with_memory_space_constraint(x, pltpu.VMEM) for x in staged]
    return pl.pallas_call(
        order_kernel,
        out_shape=jax.ShapeDtypeStruct((ROWS, COLS), F32),
        in_specs=[vmem] * 2,
        out_specs=vmem,
        scratch_shapes=[pltpu.VMEM((SECOND // 2 * 8, 2 * CH), F32)],
        compiler_params=pltpu.CompilerParams(vmem_limit_bytes=16 * 2**20),
        name="order",
    )(*staged)


def solution(mesh):
    placed = (P("lat", None, None, "lon"), P(), P(), P(), P())
    return jax.shard_map(
        per_device, mesh=mesh, in_specs=placed, out_specs=P("lat", "lon"), check_vma=False
    )
```

```python
import math

import jax
import jax.numpy as jnp
import numpy as np
from jax import lax
from jax.experimental import pallas as pl
from jax.experimental.pallas import tpu as pltpu
from jax.sharding import PartitionSpec as P

MESH = pl.DeviceIdType.MESH
BF16 = jnp.bfloat16
F32 = jnp.float32

LON_TOK = 180
PATCH = 8
NLON = 8
COLS = 180
ROWS = 16
OUT = 20
FAR_FIRST = (2, 6, 1, 7, 3, 5, 4, 0)
CH = 256
TQ = 3
CG = 8
TOK = TQ * CG
SIDES = 2
T = TQ * PATCH // SIDES
SUB = SIDES * CG
WIN = (T + 2) // 2
PAIRS = T // 2
STEP = PAIRS * SUB
SECOND = ROWS + 2
FIRST = ROWS + 4
PIX = ROWS + 6
SECOND_ORDER = tuple(range(3, 15)) + (0, 1, 2, 15, 16, 17)
ROWL = PATCH * OUT
EDGE = 512


def first_token(sector):
    return (COLS * sector - 3) // PATCH


def dft_table(mode_count):
    ids = []
    for d in range(NLON):
        for tq in range(TQ):
            for cg in range(CG):
                ids.append((first_token(d) + cg * TQ + tq) % LON_TOK)
    modes = np.arange(mode_count)
    angle = (np.array(ids)[:, None] * modes[None, :] % LON_TOK) * (2.0 * math.pi / LON_TOK)
    scale = np.where(modes == 0, 1.0, 2.0) / math.sqrt(LON_TOK)
    table = np.stack([scale * np.cos(angle), -scale * np.sin(angle)], axis=2)
    table = table.reshape(len(ids), 2 * mode_count).astype(np.float32)
    high = table.astype(BF16)
    low = (table - high.astype(np.float32)).astype(BF16)
    return np.concatenate([high, low], axis=0)


def order_table():
    table = np.zeros((2, 3 * 4 * STEP, 2 * CH), np.float32)
    for parity in range(2):
        offset = COLS * parity - PATCH * first_token(parity)
        for b in range(3):
            for q in range(COLS):
                cg, rest = divmod(q + offset - 1 + b, T * SIDES)
                side, t = divmod(rest, T)
                pair, phase = divmod(t, 2)
                at = (b * 4 + phase) * STEP + pair * SUB + side * CG + cg
                for row in range(2):
                    table[parity, at + row * 2 * STEP, row * CH + q] = 1.0
    return table.astype(BF16)


def field_kernel(
    modes_ref, table_ref, order_ref, dec_ref, in_ref, mid_ref, out_ref,
    taps, order_v,
    field, edges, halo, beyond, dec_v, in_v, mid_v, out_v, tokens, pieces, first,
    modes_s, table_s, send, in_s, mid_s, out_s, out_f,
    local_sem, dec_sem, mid_sem, send_sem, recv_sem, ready,
):
    lat, lon = lax.axis_index("lat"), lax.axis_index("lon")
    nlat = lax.axis_size("lat")
    chans = modes_s.shape[3]
    mode_count = modes_s.shape[1]

    early = [
        pltpu.make_async_copy(modes_ref, modes_s, local_sem.at[0]),
        pltpu.make_async_copy(table_ref, table_s, local_sem.at[1]),
    ]
    late = [
        pltpu.make_async_copy(in_ref, in_s, local_sem.at[2]),
        pltpu.make_async_copy(out_ref, out_s, local_sem.at[3]),
    ]
    middle = [
        pltpu.make_async_copy(
            mid_ref.at[a * 3 + b],
            mid_s.at[a] if b == 1 else mid_v.at[3 * b // 2, a * CH : (a + 1) * CH],
            mid_sem.at[a, b],
        )
        for a in range(3)
        for b in range(3)
    ]
    last = [
        pltpu.make_async_copy(
            dec_ref.at[k * chans : (k + 1) * chans], dec_v.at[k, 0:chans], dec_sem.at[k]
        )
        for k in range(NLON)
    ] + [
        pltpu.make_async_copy(order_ref.at[lax.rem(lon, 2)], order_v, local_sem.at[4]),
    ]
    for copy in early:
        copy.start()
    barrier = pltpu.get_barrier_semaphore()

    odd = lax.rem(lat, 2)
    near = lat + 1 - 2 * odd
    far = lat - 1 + 2 * odd
    has_far = (far >= 0) & (far < nlat)

    upper = jnp.minimum(lat, far)
    swap = (lax.rem(upper, 4) == 3) & (upper >= nlat // 2)
    leads = (odd == 1) != swap
    greets, greeted = has_far & leads, has_far & jnp.logical_not(leads)

    def greet(semaphore, row, column):
        there = {"lat": row, "lon": column}
        pl.semaphore_signal(semaphore, inc=1, device_id=there, device_id_type=MESH)

    @pl.when(greets)
    def _():
        for step in FAR_FIRST:
            greet(barrier, far, lax.rem(lon + step, NLON))

    for step in FAR_FIRST[:-1]:
        greet(barrier, lat, lax.rem(lon + step, NLON))
    greet(barrier, near, lon)
    for copy in late + middle + last:
        copy.start()
    send[...] = jnp.zeros_like(send)
    for copy in early:
        copy.wait()
    for row in range(2):
        values = modes_s[row].reshape(2 * mode_count, chans)
        wide = jnp.dot(table_s[...], values, preferred_element_type=F32)
        half = wide.shape[0] // 2
        whole = (wide[:half] + wide[half:]).astype(BF16)
        send[:, row, :, 0:chans] = whole.reshape(NLON, TOK, chans)
    for row in range(2):
        field[row, lon] = send[lon, row]
    pl.semaphore_wait(barrier, NLON + NLON * greeted.astype(jnp.int32))
    pl.when(greeted)(lambda: greet(ready, far, lon))

    def across(step, mine):
        there = lax.rem(lon + step, NLON)
        owner = lon if mine else lax.rem(lon + NLON - step, NLON)
        return pltpu.make_async_remote_copy(
            src_ref=send.at[there],
            dst_ref=field.at[:, owner],
            send_sem=send_sem.at[step],
            recv_sem=recv_sem.at[step],
            device_id={"lat": lat, "lon": there},
            device_id_type=MESH,
        )

    def outward(step, mine):
        owner = lon if mine else lax.rem(lon + NLON - step, NLON)
        there = lax.rem(lon + step, NLON)
        return pltpu.make_async_remote_copy(
            src_ref=send.at[there, odd],
            dst_ref=beyond.at[owner],
            send_sem=send_sem.at[NLON + 2 + step],
            recv_sem=recv_sem.at[NLON + 2 + step],
            device_id={"lat": far, "lon": there},
            device_id_type=MESH,
        )

    def onward(way, row, source, target):
        return pltpu.make_async_remote_copy(
            src_ref=edges.at[source],
            dst_ref=halo.at[target],
            send_sem=send_sem.at[NLON + way],
            recv_sem=recv_sem.at[NLON + way],
            device_id={"lat": row, "lon": lon},
            device_id_type=MESH,
        )

    to_near, from_near = (onward(0, near, 1 - odd, slot) for slot in (odd, 1 - odd))
    to_far, from_far = (onward(1, far, odd, slot) for slot in (1 - odd, odd))

    for step in FAR_FIRST[:-1]:
        across(step, True).start()

    @pl.when(greeted)
    def _():
        for step in FAR_FIRST:
            outward(step, True).start()

    @pl.when(jnp.logical_not(has_far))
    def _():
        halo[odd] = jnp.zeros(halo.shape[1:], BF16)

    for copy in late:
        copy.wait()
    dec_v[:, chans:, :] = jnp.zeros((NLON, dec_v.shape[1] - chans, dec_v.shape[2]), BF16)
    for turn in range(3):
        for phase in range(2):
            rows = []
            for place in range(3):
                a = (place - turn) % 3
                if phase:
                    rows.append(jnp.zeros((OUT, CH), BF16))
                rows += [in_s[a, b] for b in range(3)]
                if not phase:
                    rows.append(jnp.zeros((OUT, CH), BF16))
            rows.append(jnp.zeros((16, CH), BF16))
            in_v[turn, :, phase * CH : (phase + 1) * CH] = jnp.concatenate(rows, axis=0)
    out_f[...] = jnp.zeros_like(out_f)
    for a in range(3):
        for b in range(3):
            out_f[b * 8 + a : b * 8 + a + 1, :] = out_s[a, b : b + 1, :].astype(F32)
    out_v[...] = out_f[...].astype(BF16)
    for copy in middle:
        copy.wait()
    for a in range(3):
        here = slice(a * CH, (a + 1) * CH)
        ends = mid_v[0, here].astype(F32) + mid_v[3, here].astype(F32)
        centre = mid_s[a].astype(F32)
        mid_v[1, here] = (0.5 * (ends + centre)).astype(BF16)
        mid_v[2, here] = (0.5 * (ends - centre)).astype(BF16)
    for copy in last[:NLON]:
        copy.wait()
    for step in FAR_FIRST[:-1]:
        across(step, False).wait_recv()
    top, bottom = lat == 0, lat == nlat - 1
    weights = dec_v[...].reshape(NLON * 128, ROWL * PATCH)

    values = jnp.concatenate([field[:, k].reshape(2 * TOK, 128) for k in range(NLON)], axis=1)
    pixels = jnp.dot(values, weights, preferred_element_type=F32)
    edges[0] = pixels[:TOK, :EDGE].astype(BF16)
    edges[1] = pixels[TOK:, -EDGE:].astype(BF16)

    @pl.when(greets)
    def _():
        pl.semaphore_wait(ready, 1)
        to_far.start()

    to_near.start()
    tokens[1:3] = pixels.reshape(2, TQ, CG, ROWL * PATCH)

    lane = lax.broadcasted_iota(jnp.int32, (CG, CH), 1)

    def placed(slot, tq, start, place):
        base = min(start // 128 * 128, ROWL * PATCH - CH)
        block = tokens[slot, tq, :, base : base + CH]
        shift = (place - (start - base)) % CH
        return pltpu.roll(block, shift, 1) if shift else block

    def half(p, w):
        slot, pr, place = p // PATCH + 1, p % PATCH, p % 3 * 80
        tq, part = divmod(w, 4)
        if part:
            return placed(slot, tq, pr * ROWL + (part - 1) * 40, place)
        before = placed(slot, (tq - 1) % TQ, pr * ROWL + 120, place)
        own = placed(slot, tq % TQ, pr * ROWL, place + 40)
        if tq == 0:
            before = pltpu.roll(before, 1, 0)
        if tq == TQ:
            own = pltpu.roll(own, CG - 1, 0)
        return jnp.where(lane < place + 40, before, own)

    def spread(rows):
        for i in rows:
            values = [half(i - 3, w) for w in range(SIDES * PAIRS + 1)]
            for w in range(WIN):
                pieces[i, w] = jnp.concatenate([values[w], values[w + PAIRS]], axis=0).astype(BF16)

    lane2 = lax.broadcasted_iota(jnp.int32, (SUB, CH), 1)

    def first_rows(rows):
        for turn in range(3):
            mine = [j for j in rows if j % 3 == turn]
            windows = []
            for j in mine:
                parts = [pieces[j + (c - j) % 3] for c in range(3)]
                window = jnp.where(lane2 < 80, parts[0], jnp.where(lane2 < 160, parts[1], parts[2]))
                windows.append(window.reshape(WIN * SUB, CH))
            hidden = jnp.maximum(
                jnp.dot(
                    jnp.concatenate(windows, axis=0), in_v[turn], preferred_element_type=F32
                ),
                0.0,
            ).reshape(len(mine), WIN, SUB, 2 * CH)
            for at, j in enumerate(mine):
                left, right = hidden[at, :, :, :CH], hidden[at, :, :, CH:]
                if j < 2 or j >= FIRST - 2:
                    outside = top if j < 2 else bottom
                    left = jnp.where(outside, 0.0, left)
                    right = jnp.where(outside, 0.0, right)
                here = slice(j * STEP, (j + 1) * STEP)
                first[0, here] = (left[:-1] - left[1:]).reshape(STEP, CH).astype(BF16)
                first[1, here] = (right[:-1] + left[1:]).reshape(STEP, CH).astype(BF16)
                first[2, here] = (left[1:] - right[:-1]).reshape(STEP, CH).astype(BF16)
                first[3, here] = (right[:-1] - right[1:]).reshape(STEP, CH).astype(BF16)

    def second_rows(low, count):
        products = []
        for k in range(4):
            blocks = [first[k, (low + a) * STEP : (low + a + count) * STEP] for a in range(3)]
            products.append(
                jnp.dot(jnp.concatenate(blocks, axis=1), mid_v[k], preferred_element_type=F32)
            )
        pair = (
            products[0] + (products[1] + products[2]),
            (products[1] - products[2]) - products[3],
        )
        pair = [jnp.maximum(x, 0.0).reshape(count, STEP, CH) for x in pair]
        rows = []
        for step in range(count):
            values = [x[step] for x in pair]
            if low + step == 0:
                values = [jnp.where(top, 0.0, x) for x in values]
            if low + step == SECOND - 1:
                values = [jnp.where(bottom, 0.0, x) for x in values]
            rows += [x.astype(BF16) for x in values]
        return rows

    def last_taps(rows, slot):
        for i in range(0, len(rows), 4):
            tap = lax.dot_general(
                out_v[...],
                jnp.concatenate(rows[i : i + 4], axis=0),
                (((1,), (1,)), ((), ())),
                preferred_element_type=F32,
            )
            taps[slot + i // 4] = jnp.concatenate([tap[b * 8 : b * 8 + 8] for b in range(3)], axis=1)

    spread(range(3, 19))
    first_rows(range(3, 17))
    last_taps(second_rows(3, 6), 0)
    last_taps(second_rows(9, 6), 3)

    from_near.wait_recv()
    pl.when(greeted)(lambda: from_far.wait_recv())

    def decode(side, lanes):
        row = jnp.concatenate([beyond[k] for k in range(NLON)], axis=1)
        part = dec_v[:, :, lanes].reshape(NLON * 128, EDGE)
        halo[side] = jnp.dot(row, part, preferred_element_type=F32).astype(BF16)

    @pl.when(greets)
    def _():
        for step in FAR_FIRST:
            outward(step, False).wait_recv()
        pl.when(odd == 0)(lambda: decode(0, slice(ROWL * PATCH - EDGE, ROWL * PATCH)))
        pl.when(odd == 1)(lambda: decode(1, slice(0, EDGE)))

    tokens[0, :, :, -EDGE:] = halo[0].astype(F32).reshape(TQ, CG, EDGE)
    tokens[3, :, :, :EDGE] = halo[1].astype(F32).reshape(TQ, CG, EDGE)
    spread((0, 1, 2, 19, 20, 21))
    first_rows((0, 1, 2, 17, 18, 19))
    last_taps(second_rows(0, 3) + second_rows(15, 3), 6)

    for copy in last[NLON:]:
        copy.wait()
    for step in FAR_FIRST[:-1]:
        across(step, True).wait_send()
    to_near.wait_send()
    pl.when(greets)(lambda: to_far.wait_send())

    @pl.when(greeted)
    def _():
        for step in FAR_FIRST:
            outward(step, True).wait_send()


def order_kernel(taps, order_v, result, sums):
    count = taps.shape[0] * 8
    tap = taps[...].reshape(count, 3 * 4 * STEP)
    high = tap.astype(BF16)
    low = (tap - high.astype(F32)).astype(BF16)
    moved = jnp.dot(
        jnp.concatenate([high, low], axis=0), order_v[...], preferred_element_type=F32
    )
    sums[...] = moved[:count] + moved[count:]
    for p in range(ROWS):
        total = None
        for a in range(3):
            slot, half = divmod(SECOND_ORDER.index(p + a), 2)
            term = sums[slot * 8 + a : slot * 8 + a + 1, half * CH : half * CH + COLS]
            total = term if total is None else total + term
        result[p : p + 1, :] = total


def per_device(kept_modes, decoder_weight, conv_in_weight, conv_mid_weight, conv_out_weight):
    mode_count, chans = kept_modes.shape[1], kept_modes.shape[3]
    table = dft_table(mode_count)
    order = order_table()
    vmem = pl.BlockSpec(memory_space=pltpu.VMEM)
    dma = pltpu.SemaphoreType.DMA
    staged = pl.pallas_call(
        field_kernel,
        out_shape=(
            pltpu.VMEM((SECOND // 2, 8, 3 * 4 * STEP), F32),
            pltpu.VMEM(order.shape[1:], BF16),
        ),
        in_specs=[pl.BlockSpec(memory_space=pltpu.HBM)] * 7,
        out_specs=(vmem,) * 2,
        scratch_shapes=[
            pltpu.VMEM((2, NLON, TOK, 128), BF16),
            pltpu.VMEM((2, TOK, EDGE), BF16),
            pltpu.VMEM((2, TOK, EDGE), BF16),
            pltpu.VMEM((NLON, TOK, 128), BF16),
            pltpu.VMEM((NLON, 128, ROWL * PATCH), BF16),
            pltpu.VMEM((3, CH, 2 * CH), BF16),
            pltpu.VMEM((4, 3 * CH, CH), BF16),
            pltpu.VMEM((24, CH), BF16),
            pltpu.VMEM((4, TQ, CG, ROWL * PATCH), F32),
            pltpu.VMEM((PIX, WIN, SUB, CH), BF16),
            pltpu.VMEM((4, FIRST * STEP, CH), BF16),
            pltpu.VMEM(kept_modes.shape, BF16),
            pltpu.VMEM(table.shape, BF16),
            pltpu.VMEM((NLON, 2, TOK, 128), BF16),
            pltpu.VMEM(conv_in_weight.shape, BF16),
            pltpu.VMEM((3, CH, CH), BF16),
            pltpu.VMEM((3, 3, CH), BF16),
            pltpu.VMEM((24, CH), F32),
            dma((5,)),
            dma((NLON,)),
            dma((3, 3)),
            dma((2 * NLON + 2,)),
            dma((2 * NLON + 2,)),
            pltpu.SemaphoreType.REGULAR,
        ],
        compiler_params=pltpu.CompilerParams(
            collective_id=0, has_side_effects=True, vmem_limit_bytes=40 * 2**20
        ),
        name="field_to_taps",
    )(
        *[
            pltpu.with_memory_space_constraint(x, pltpu.HBM)
            for x in (
                kept_modes,
                jnp.asarray(table),
                jnp.asarray(order),
                decoder_weight,
                conv_in_weight,
                conv_mid_weight.reshape(9, CH, CH),
                conv_out_weight.reshape(3, 3, CH),
            )
        ]
    )
    staged = [pltpu.with_memory_space_constraint(x, pltpu.VMEM) for x in staged]
    return pl.pallas_call(
        order_kernel,
        out_shape=jax.ShapeDtypeStruct((ROWS, COLS), F32),
        in_specs=[vmem] * 2,
        out_specs=vmem,
        scratch_shapes=[pltpu.VMEM((SECOND // 2 * 8, 2 * CH), F32)],
        compiler_params=pltpu.CompilerParams(vmem_limit_bytes=16 * 2**20),
        name="order",
    )(*staged)


def solution(mesh):
    placed = (P("lat", None, None, "lon"), P(), P(), P(), P())
    return jax.shard_map(
        per_device, mesh=mesh, in_specs=placed, out_specs=P("lat", "lon"), check_vma=False
    )
```

```python
import math

import jax
import jax.numpy as jnp
import numpy as np
from jax import lax
from jax.experimental import pallas as pl
from jax.experimental.pallas import tpu as pltpu
from jax.sharding import PartitionSpec as P

MESH = pl.DeviceIdType.MESH
BF16 = jnp.bfloat16
F32 = jnp.float32

LON_TOK = 180
PATCH = 8
NLON = 8
COLS = 180
ROWS = 16
OUT = 20
FAR_FIRST = (2, 6, 1, 7, 3, 5, 4, 0)
CH = 256
TQ = 3
CG = 8
TOK = TQ * CG
SIDES = 2
T = TQ * PATCH // SIDES
SUB = SIDES * CG
WIN = (T + 2) // 2
PAIRS = T // 2
STEP = PAIRS * SUB
SECOND = ROWS + 2
FIRST = ROWS + 4
PIX = ROWS + 6
SECOND_ORDER = tuple(range(3, 15)) + (0, 1, 2, 15, 16, 17)
ROWL = PATCH * OUT
EDGE = 512


def first_token(sector):
    return (COLS * sector - 3) // PATCH


def dft_table(mode_count):
    ids = []
    for d in range(NLON):
        for tq in range(TQ):
            for cg in range(CG):
                ids.append((first_token(d) + cg * TQ + tq) % LON_TOK)
    modes = np.arange(mode_count)
    angle = (np.array(ids)[:, None] * modes[None, :] % LON_TOK) * (2.0 * math.pi / LON_TOK)
    scale = np.where(modes == 0, 1.0, 2.0) / math.sqrt(LON_TOK)
    table = np.stack([scale * np.cos(angle), -scale * np.sin(angle)], axis=2)
    table = table.reshape(len(ids), 2 * mode_count).astype(np.float32)
    high = table.astype(BF16)
    low = (table - high.astype(np.float32)).astype(BF16)
    return np.concatenate([high, low], axis=0)


def order_table():
    table = np.zeros((2, 3 * 4 * STEP, 2 * CH), np.float32)
    for parity in range(2):
        offset = COLS * parity - PATCH * first_token(parity)
        for b in range(3):
            for q in range(COLS):
                cg, rest = divmod(q + offset - 1 + b, T * SIDES)
                side, t = divmod(rest, T)
                pair, phase = divmod(t, 2)
                at = (b * 4 + phase) * STEP + pair * SUB + side * CG + cg
                for row in range(2):
                    table[parity, at + row * 2 * STEP, row * CH + q] = 1.0
    return table.astype(BF16)


def field_kernel(
    modes_ref, table_ref, order_ref, dec_ref, in_ref, mid_ref, out_ref,
    taps, order_v,
    field, edges, halo, beyond, dec_v, in_v, mid_v, out_v, tokens, pieces, first,
    modes_s, table_s, send, in_s, mid_s, out_s, out_f,
    local_sem, dec_sem, mid_sem, send_sem, recv_sem, ready,
):
    lat, lon = lax.axis_index("lat"), lax.axis_index("lon")
    nlat = lax.axis_size("lat")
    chans = modes_s.shape[3]
    mode_count = modes_s.shape[1]

    early = [
        pltpu.make_async_copy(modes_ref, modes_s, local_sem.at[0]),
        pltpu.make_async_copy(table_ref, table_s, local_sem.at[1]),
    ]
    late = [
        pltpu.make_async_copy(in_ref, in_s, local_sem.at[2]),
        pltpu.make_async_copy(out_ref, out_s, local_sem.at[3]),
    ]
    middle = [
        pltpu.make_async_copy(
            mid_ref.at[a * 3 + b],
            mid_s.at[a] if b == 1 else mid_v.at[3 * b // 2, a * CH : (a + 1) * CH],
            mid_sem.at[a, b],
        )
        for a in range(3)
        for b in range(3)
    ]
    last = [
        pltpu.make_async_copy(
            dec_ref.at[k * chans : (k + 1) * chans], dec_v.at[k, 0:chans], dec_sem.at[k]
        )
        for k in range(NLON)
    ] + [
        pltpu.make_async_copy(order_ref.at[lax.rem(lon, 2)], order_v, local_sem.at[4]),
    ]
    for copy in early:
        copy.start()
    barrier = pltpu.get_barrier_semaphore()

    odd = lax.rem(lat, 2)
    near = lat + 1 - 2 * odd
    far = lat - 1 + 2 * odd
    has_far = (far >= 0) & (far < nlat)

    upper = jnp.minimum(lat, far)
    swap = (lax.rem(upper, 4) == 3) & (upper >= nlat // 2)
    leads = (odd == 1) != swap
    greets, greeted = has_far & leads, has_far & jnp.logical_not(leads)

    def greet(semaphore, row, column):
        there = {"lat": row, "lon": column}
        pl.semaphore_signal(semaphore, inc=1, device_id=there, device_id_type=MESH)

    for step in FAR_FIRST[:-1]:
        greet(barrier, lat, lax.rem(lon + step, NLON))

    @pl.when(greets)
    def _():
        for step in FAR_FIRST:
            greet(barrier, far, lax.rem(lon + step, NLON))

    greet(barrier, near, lon)
    for copy in late + middle + last:
        copy.start()
    send[...] = jnp.zeros_like(send)
    for copy in early:
        copy.wait()
    for row in range(2):
        values = modes_s[row].reshape(2 * mode_count, chans)
        wide = jnp.dot(table_s[...], values, preferred_element_type=F32)
        half = wide.shape[0] // 2
        whole = (wide[:half] + wide[half:]).astype(BF16)
        send[:, row, :, 0:chans] = whole.reshape(NLON, TOK, chans)
    for row in range(2):
        field[row, lon] = send[lon, row]
    pl.semaphore_wait(barrier, NLON + NLON * greeted.astype(jnp.int32))
    pl.when(greeted)(lambda: greet(ready, far, lon))

    def across(step, mine):
        there = lax.rem(lon + step, NLON)
        owner = lon if mine else lax.rem(lon + NLON - step, NLON)
        return pltpu.make_async_remote_copy(
            src_ref=send.at[there],
            dst_ref=field.at[:, owner],
            send_sem=send_sem.at[step],
            recv_sem=recv_sem.at[step],
            device_id={"lat": lat, "lon": there},
            device_id_type=MESH,
        )

    def outward(step, mine):
        owner = lon if mine else lax.rem(lon + NLON - step, NLON)
        there = lax.rem(lon + step, NLON)
        return pltpu.make_async_remote_copy(
            src_ref=send.at[there, odd],
            dst_ref=beyond.at[owner],
            send_sem=send_sem.at[NLON + 2 + step],
            recv_sem=recv_sem.at[NLON + 2 + step],
            device_id={"lat": far, "lon": there},
            device_id_type=MESH,
        )

    def onward(way, row, source, target):
        return pltpu.make_async_remote_copy(
            src_ref=edges.at[source],
            dst_ref=halo.at[target],
            send_sem=send_sem.at[NLON + way],
            recv_sem=recv_sem.at[NLON + way],
            device_id={"lat": row, "lon": lon},
            device_id_type=MESH,
        )

    to_near, from_near = (onward(0, near, 1 - odd, slot) for slot in (odd, 1 - odd))
    to_far, from_far = (onward(1, far, odd, slot) for slot in (1 - odd, odd))

    for step in FAR_FIRST[:-1]:
        across(step, True).start()

    @pl.when(greeted)
    def _():
        for step in FAR_FIRST:
            outward(step, True).start()

    @pl.when(jnp.logical_not(has_far))
    def _():
        halo[odd] = jnp.zeros(halo.shape[1:], BF16)

    for copy in late:
        copy.wait()
    dec_v[:, chans:, :] = jnp.zeros((NLON, dec_v.shape[1] - chans, dec_v.shape[2]), BF16)
    for turn in range(3):
        for phase in range(2):
            rows = []
            for place in range(3):
                a = (place - turn) % 3
                if phase:
                    rows.append(jnp.zeros((OUT, CH), BF16))
                rows += [in_s[a, b] for b in range(3)]
                if not phase:
                    rows.append(jnp.zeros((OUT, CH), BF16))
            rows.append(jnp.zeros((16, CH), BF16))
            in_v[turn, :, phase * CH : (phase + 1) * CH] = jnp.concatenate(rows, axis=0)
    out_f[...] = jnp.zeros_like(out_f)
    for a in range(3):
        for b in range(3):
            out_f[b * 8 + a : b * 8 + a + 1, :] = out_s[a, b : b + 1, :].astype(F32)
    out_v[...] = out_f[...].astype(BF16)
    for copy in middle:
        copy.wait()
    for a in range(3):
        here = slice(a * CH, (a + 1) * CH)
        ends = mid_v[0, here].astype(F32) + mid_v[3, here].astype(F32)
        centre = mid_s[a].astype(F32)
        mid_v[1, here] = (0.5 * (ends + centre)).astype(BF16)
        mid_v[2, here] = (0.5 * (ends - centre)).astype(BF16)
    for copy in last[:NLON]:
        copy.wait()
    top, bottom = lat == 0, lat == nlat - 1
    pixels = None
    for group in ((0, 4), (3, 5), (1, 7), (2, 6)):
        rows, weights = [], []
        for step in group:
            if step:
                across(step, False).wait_recv()
            origin = lax.rem(lon + NLON - step, NLON)
            rows.append(field[:, origin].reshape(2 * TOK, 128))
            weights.append(dec_v[origin])
        part = jnp.dot(
            jnp.concatenate(rows, axis=1),
            jnp.concatenate(weights, axis=0),
            preferred_element_type=F32,
        )
        pixels = part if pixels is None else pixels + part
    edges[0] = pixels[:TOK, :EDGE].astype(BF16)
    edges[1] = pixels[TOK:, -EDGE:].astype(BF16)

    @pl.when(greets)
    def _():
        pl.semaphore_wait(ready, 1)
        to_far.start()

    to_near.start()
    tokens[1:3] = pixels.reshape(2, TQ, CG, ROWL * PATCH)

    lane = lax.broadcasted_iota(jnp.int32, (CG, CH), 1)

    def placed(slot, tq, start, place):
        base = min(start // 128 * 128, ROWL * PATCH - CH)
        block = tokens[slot, tq, :, base : base + CH]
        shift = (place - (start - base)) % CH
        return pltpu.roll(block, shift, 1) if shift else block

    def half(p, w):
        slot, pr, place = p // PATCH + 1, p % PATCH, p % 3 * 80
        tq, part = divmod(w, 4)
        if part:
            return placed(slot, tq, pr * ROWL + (part - 1) * 40, place)
        before = placed(slot, (tq - 1) % TQ, pr * ROWL + 120, place)
        own = placed(slot, tq % TQ, pr * ROWL, place + 40)
        if tq == 0:
            before = pltpu.roll(before, 1, 0)
        if tq == TQ:
            own = pltpu.roll(own, CG - 1, 0)
        return jnp.where(lane < place + 40, before, own)

    def spread(rows):
        for i in rows:
            values = [half(i - 3, w) for w in range(SIDES * PAIRS + 1)]
            for w in range(WIN):
                pieces[i, w] = jnp.concatenate([values[w], values[w + PAIRS]], axis=0).astype(BF16)

    lane2 = lax.broadcasted_iota(jnp.int32, (SUB, CH), 1)

    def first_rows(rows):
        for turn in range(3):
            mine = [j for j in rows if j % 3 == turn]
            windows = []
            for j in mine:
                parts = [pieces[j + (c - j) % 3] for c in range(3)]
                window = jnp.where(lane2 < 80, parts[0], jnp.where(lane2 < 160, parts[1], parts[2]))
                windows.append(window.reshape(WIN * SUB, CH))
            hidden = jnp.maximum(
                jnp.dot(
                    jnp.concatenate(windows, axis=0), in_v[turn], preferred_element_type=F32
                ),
                0.0,
            ).reshape(len(mine), WIN, SUB, 2 * CH)
            for at, j in enumerate(mine):
                left, right = hidden[at, :, :, :CH], hidden[at, :, :, CH:]
                if j < 2 or j >= FIRST - 2:
                    outside = top if j < 2 else bottom
                    left = jnp.where(outside, 0.0, left)
                    right = jnp.where(outside, 0.0, right)
                here = slice(j * STEP, (j + 1) * STEP)
                first[0, here] = (left[:-1] - left[1:]).reshape(STEP, CH).astype(BF16)
                first[1, here] = (right[:-1] + left[1:]).reshape(STEP, CH).astype(BF16)
                first[2, here] = (left[1:] - right[:-1]).reshape(STEP, CH).astype(BF16)
                first[3, here] = (right[:-1] - right[1:]).reshape(STEP, CH).astype(BF16)

    def second_rows(*spans):
        order = [i for low, high in spans for i in range(low, high)]
        count = len(order)
        products = []
        for k in range(4):
            blocks = []
            for a in range(3):
                parts = [first[k, (low + a) * STEP : (high + a) * STEP] for low, high in spans]
                blocks.append(jnp.concatenate(parts, axis=0))
            products.append(
                jnp.dot(jnp.concatenate(blocks, axis=1), mid_v[k], preferred_element_type=F32)
            )
        pair = (
            products[0] + (products[1] + products[2]),
            (products[1] - products[2]) - products[3],
        )
        pair = [jnp.maximum(x, 0.0).reshape(count, STEP, CH) for x in pair]
        rows = []
        for step, i in enumerate(order):
            values = [x[step] for x in pair]
            if i == 0:
                values = [jnp.where(top, 0.0, x) for x in values]
            if i == SECOND - 1:
                values = [jnp.where(bottom, 0.0, x) for x in values]
            rows += [x.astype(BF16) for x in values]
        return rows

    def last_taps(rows, slot):
        tap = lax.dot_general(
            out_v[...],
            jnp.concatenate(rows, axis=0),
            (((1,), (1,)), ((), ())),
            preferred_element_type=F32,
        )
        for i in range(len(rows) // 4):
            part = tap[:, i * 4 * STEP : (i + 1) * 4 * STEP]
            taps[slot + i] = jnp.concatenate([part[b * 8 : b * 8 + 8] for b in range(3)], axis=1)

    spread(range(3, 19))
    first_rows(range(3, 17))
    last_taps(second_rows((3, 15)), 0)

    from_near.wait_recv()
    pl.when(greeted)(lambda: from_far.wait_recv())

    def decode(side, lanes):
        row = jnp.concatenate([beyond[k] for k in range(NLON)], axis=1)
        part = dec_v[:, :, lanes].reshape(NLON * 128, EDGE)
        halo[side] = jnp.dot(row, part, preferred_element_type=F32).astype(BF16)

    @pl.when(greets)
    def _():
        for step in FAR_FIRST:
            outward(step, False).wait_recv()
        pl.when(odd == 0)(lambda: decode(0, slice(ROWL * PATCH - EDGE, ROWL * PATCH)))
        pl.when(odd == 1)(lambda: decode(1, slice(0, EDGE)))

    tokens[0, :, :, -EDGE:] = halo[0].astype(F32).reshape(TQ, CG, EDGE)
    tokens[3, :, :, :EDGE] = halo[1].astype(F32).reshape(TQ, CG, EDGE)
    spread((0, 1, 2, 19, 20, 21))
    first_rows((0, 1, 2, 17, 18, 19))
    last_taps(second_rows((0, 3), (15, 18)), 6)

    for copy in last[NLON:]:
        copy.wait()
    for step in FAR_FIRST[:-1]:
        across(step, True).wait_send()
    to_near.wait_send()
    pl.when(greets)(lambda: to_far.wait_send())

    @pl.when(greeted)
    def _():
        for step in FAR_FIRST:
            outward(step, True).wait_send()


def order_kernel(taps, order_v, result, sums):
    count = taps.shape[0] * 8
    tap = taps[...].reshape(count, 3 * 4 * STEP)
    high = tap.astype(BF16)
    low = (tap - high.astype(F32)).astype(BF16)
    moved = jnp.dot(
        jnp.concatenate([high, low], axis=0), order_v[...], preferred_element_type=F32
    )
    sums[...] = moved[:count] + moved[count:]
    for p in range(ROWS):
        total = None
        for a in range(3):
            slot, half = divmod(SECOND_ORDER.index(p + a), 2)
            term = sums[slot * 8 + a : slot * 8 + a + 1, half * CH : half * CH + COLS]
            total = term if total is None else total + term
        result[p : p + 1, :] = total


def per_device(kept_modes, decoder_weight, conv_in_weight, conv_mid_weight, conv_out_weight):
    mode_count, chans = kept_modes.shape[1], kept_modes.shape[3]
    table = dft_table(mode_count)
    order = order_table()
    vmem = pl.BlockSpec(memory_space=pltpu.VMEM)
    dma = pltpu.SemaphoreType.DMA
    staged = pl.pallas_call(
        field_kernel,
        out_shape=(
            pltpu.VMEM((SECOND // 2, 8, 3 * 4 * STEP), F32),
            pltpu.VMEM(order.shape[1:], BF16),
        ),
        in_specs=[pl.BlockSpec(memory_space=pltpu.HBM)] * 7,
        out_specs=(vmem,) * 2,
        scratch_shapes=[
            pltpu.VMEM((2, NLON, TOK, 128), BF16),
            pltpu.VMEM((2, TOK, EDGE), BF16),
            pltpu.VMEM((2, TOK, EDGE), BF16),
            pltpu.VMEM((NLON, TOK, 128), BF16),
            pltpu.VMEM((NLON, 128, ROWL * PATCH), BF16),
            pltpu.VMEM((3, CH, 2 * CH), BF16),
            pltpu.VMEM((4, 3 * CH, CH), BF16),
            pltpu.VMEM((24, CH), BF16),
            pltpu.VMEM((4, TQ, CG, ROWL * PATCH), F32),
            pltpu.VMEM((PIX, WIN, SUB, CH), BF16),
            pltpu.VMEM((4, FIRST * STEP, CH), BF16),
            pltpu.VMEM(kept_modes.shape, BF16),
            pltpu.VMEM(table.shape, BF16),
            pltpu.VMEM((NLON, 2, TOK, 128), BF16),
            pltpu.VMEM(conv_in_weight.shape, BF16),
            pltpu.VMEM((3, CH, CH), BF16),
            pltpu.VMEM((3, 3, CH), BF16),
            pltpu.VMEM((24, CH), F32),
            dma((5,)),
            dma((NLON,)),
            dma((3, 3)),
            dma((2 * NLON + 2,)),
            dma((2 * NLON + 2,)),
            pltpu.SemaphoreType.REGULAR,
        ],
        compiler_params=pltpu.CompilerParams(
            collective_id=0, has_side_effects=True, vmem_limit_bytes=40 * 2**20
        ),
        name="field_to_taps",
    )(
        *[
            pltpu.with_memory_space_constraint(x, pltpu.HBM)
            for x in (
                kept_modes,
                jnp.asarray(table),
                jnp.asarray(order),
                decoder_weight,
                conv_in_weight,
                conv_mid_weight.reshape(9, CH, CH),
                conv_out_weight.reshape(3, 3, CH),
            )
        ]
    )
    staged = [pltpu.with_memory_space_constraint(x, pltpu.VMEM) for x in staged]
    return pl.pallas_call(
        order_kernel,
        out_shape=jax.ShapeDtypeStruct((ROWS, COLS), F32),
        in_specs=[vmem] * 2,
        out_specs=vmem,
        scratch_shapes=[pltpu.VMEM((SECOND // 2 * 8, 2 * CH), F32)],
        compiler_params=pltpu.CompilerParams(vmem_limit_bytes=16 * 2**20),
        name="order",
    )(*staged)


def solution(mesh):
    placed = (P("lat", None, None, "lon"), P(), P(), P(), P())
    return jax.shard_map(
        per_device, mesh=mesh, in_specs=placed, out_specs=P("lat", "lon"), check_vma=False
    )
```

```python
import math

import jax
import jax.numpy as jnp
import numpy as np
from jax import lax
from jax.experimental import pallas as pl
from jax.experimental.pallas import tpu as pltpu
from jax.sharding import PartitionSpec as P

MESH = pl.DeviceIdType.MESH
BF16 = jnp.bfloat16
F32 = jnp.float32

LON_TOK = 180
PATCH = 8
NLON = 8
COLS = 180
ROWS = 16
OUT = 20
FAR_FIRST = (2, 6, 1, 7, 3, 5, 4, 0)
CH = 256
TQ = 3
CG = 8
TOK = TQ * CG
SIDES = 2
T = TQ * PATCH // SIDES
SUB = SIDES * CG
WIN = (T + 2) // 2
PAIRS = T // 2
STEP = PAIRS * SUB
SECOND = ROWS + 2
FIRST = ROWS + 4
PIX = ROWS + 6
SECOND_ORDER = tuple(range(3, 15)) + (0, 1, 2, 15, 16, 17)
ROWL = PATCH * OUT
EDGE = 512


def first_token(sector):
    return (COLS * sector - 3) // PATCH


def dft_table(mode_count):
    ids = []
    for d in range(NLON):
        for tq in range(TQ):
            for cg in range(CG):
                ids.append((first_token(d) + cg * TQ + tq) % LON_TOK)
    modes = np.arange(mode_count)
    angle = (np.array(ids)[:, None] * modes[None, :] % LON_TOK) * (2.0 * math.pi / LON_TOK)
    scale = np.where(modes == 0, 1.0, 2.0) / math.sqrt(LON_TOK)
    table = np.stack([scale * np.cos(angle), -scale * np.sin(angle)], axis=2)
    table = table.reshape(len(ids), 2 * mode_count).astype(np.float32)
    high = table.astype(BF16)
    low = (table - high.astype(np.float32)).astype(BF16)
    return np.concatenate([high, low], axis=0)


def order_table():
    table = np.zeros((2, 3 * 4 * STEP, 2 * CH), np.float32)
    for parity in range(2):
        offset = COLS * parity - PATCH * first_token(parity)
        for b in range(3):
            for q in range(COLS):
                cg, rest = divmod(q + offset - 1 + b, T * SIDES)
                side, t = divmod(rest, T)
                pair, phase = divmod(t, 2)
                at = (b * 4 + phase) * STEP + pair * SUB + side * CG + cg
                for row in range(2):
                    table[parity, at + row * 2 * STEP, row * CH + q] = 1.0
    return table.astype(BF16)


def field_kernel(
    modes_ref, table_ref, order_ref, dec_ref, in_ref, mid_ref, out_ref,
    taps, order_v,
    field, edges, halo, beyond, dec_v, in_v, mid_v, out_v, tokens, pieces, first,
    modes_s, table_s, send, in_s, mid_s, out_s, out_f,
    local_sem, dec_sem, mid_sem, send_sem, recv_sem, ready,
):
    lat, lon = lax.axis_index("lat"), lax.axis_index("lon")
    nlat = lax.axis_size("lat")
    chans = modes_s.shape[3]
    mode_count = modes_s.shape[1]

    early = [
        pltpu.make_async_copy(modes_ref, modes_s, local_sem.at[0]),
        pltpu.make_async_copy(table_ref, table_s, local_sem.at[1]),
    ]
    late = [
        pltpu.make_async_copy(in_ref, in_s, local_sem.at[2]),
        pltpu.make_async_copy(out_ref, out_s, local_sem.at[3]),
    ]
    middle = [
        pltpu.make_async_copy(
            mid_ref.at[a * 3 + b],
            mid_s.at[a] if b == 1 else mid_v.at[3 * b // 2, a * CH : (a + 1) * CH],
            mid_sem.at[a, b],
        )
        for a in range(3)
        for b in range(3)
    ]
    last = [
        pltpu.make_async_copy(
            dec_ref.at[k * chans : (k + 1) * chans], dec_v.at[k, 0:chans], dec_sem.at[k]
        )
        for k in range(NLON)
    ] + [
        pltpu.make_async_copy(order_ref.at[lax.rem(lon, 2)], order_v, local_sem.at[4]),
    ]
    barrier = pltpu.get_barrier_semaphore()

    odd = lax.rem(lat, 2)
    near = lat + 1 - 2 * odd
    far = lat - 1 + 2 * odd
    has_far = (far >= 0) & (far < nlat)

    upper = jnp.minimum(lat, far)
    swap = (lax.rem(upper, 4) == 3) & (upper >= nlat // 2)
    leads = (odd == 1) != swap
    greets, greeted = has_far & leads, has_far & jnp.logical_not(leads)

    def greet(semaphore, row, column):
        there = {"lat": row, "lon": column}
        pl.semaphore_signal(semaphore, inc=1, device_id=there, device_id_type=MESH)

    @pl.when(greets)
    def _():
        for step in FAR_FIRST:
            greet(barrier, far, lax.rem(lon + step, NLON))

    for step in FAR_FIRST[:-1]:
        greet(barrier, lat, lax.rem(lon + step, NLON))

    greet(barrier, near, lon)
    for copy in early:
        copy.start()
    for copy in late + middle + last:
        copy.start()
    send[...] = jnp.zeros_like(send)
    for copy in early:
        copy.wait()
    for row in range(2):
        values = modes_s[row].reshape(2 * mode_count, chans)
        wide = jnp.dot(table_s[...], values, preferred_element_type=F32)
        half = wide.shape[0] // 2
        whole = (wide[:half] + wide[half:]).astype(BF16)
        send[:, row, :, 0:chans] = whole.reshape(NLON, TOK, chans)
    for row in range(2):
        field[row, lon] = send[lon, row]
    pl.semaphore_wait(barrier, NLON + NLON * greeted.astype(jnp.int32))
    pl.when(greeted)(lambda: greet(ready, far, lon))

    def across(step, mine):
        there = lax.rem(lon + step, NLON)
        owner = lon if mine else lax.rem(lon + NLON - step, NLON)
        return pltpu.make_async_remote_copy(
            src_ref=send.at[there],
            dst_ref=field.at[:, owner],
            send_sem=send_sem.at[step],
            recv_sem=recv_sem.at[step],
            device_id={"lat": lat, "lon": there},
            device_id_type=MESH,
        )

    def outward(step, mine):
        owner = lon if mine else lax.rem(lon + NLON - step, NLON)
        there = lax.rem(lon + step, NLON)
        return pltpu.make_async_remote_copy(
            src_ref=send.at[there, odd],
            dst_ref=beyond.at[owner],
            send_sem=send_sem.at[NLON + 2 + step],
            recv_sem=recv_sem.at[NLON + 2 + step],
            device_id={"lat": far, "lon": there},
            device_id_type=MESH,
        )

    def onward(way, row, source, target):
        return pltpu.make_async_remote_copy(
            src_ref=edges.at[source],
            dst_ref=halo.at[target],
            send_sem=send_sem.at[NLON + way],
            recv_sem=recv_sem.at[NLON + way],
            device_id={"lat": row, "lon": lon},
            device_id_type=MESH,
        )

    to_near, from_near = (onward(0, near, 1 - odd, slot) for slot in (odd, 1 - odd))
    to_far, from_far = (onward(1, far, odd, slot) for slot in (1 - odd, odd))

    for step in FAR_FIRST[:-1]:
        across(step, True).start()

    @pl.when(greeted)
    def _():
        for step in FAR_FIRST:
            outward(step, True).start()

    @pl.when(jnp.logical_not(has_far))
    def _():
        halo[odd] = jnp.zeros(halo.shape[1:], BF16)

    for copy in late:
        copy.wait()
    dec_v[:, chans:, :] = jnp.zeros((NLON, dec_v.shape[1] - chans, dec_v.shape[2]), BF16)
    for turn in range(3):
        for phase in range(2):
            rows = []
            for place in range(3):
                a = (place - turn) % 3
                if phase:
                    rows.append(jnp.zeros((OUT, CH), BF16))
                rows += [in_s[a, b] for b in range(3)]
                if not phase:
                    rows.append(jnp.zeros((OUT, CH), BF16))
            rows.append(jnp.zeros((16, CH), BF16))
            in_v[turn, :, phase * CH : (phase + 1) * CH] = jnp.concatenate(rows, axis=0)
    out_f[...] = jnp.zeros_like(out_f)
    for a in range(3):
        for b in range(3):
            out_f[b * 8 + a : b * 8 + a + 1, :] = out_s[a, b : b + 1, :].astype(F32)
    out_v[...] = out_f[...].astype(BF16)
    for copy in middle:
        copy.wait()
    for a in range(3):
        here = slice(a * CH, (a + 1) * CH)
        ends = mid_v[0, here].astype(F32) + mid_v[3, here].astype(F32)
        centre = mid_s[a].astype(F32)
        mid_v[1, here] = (0.5 * (ends + centre)).astype(BF16)
        mid_v[2, here] = (0.5 * (ends - centre)).astype(BF16)
    for copy in last[:NLON]:
        copy.wait()
    top, bottom = lat == 0, lat == nlat - 1
    pixels = None
    for group in ((0, 4), (3, 5), (1, 7), (2, 6)):
        rows, weights = [], []
        for step in group:
            if step:
                across(step, False).wait_recv()
            origin = lax.rem(lon + NLON - step, NLON)
            rows.append(field[:, origin].reshape(2 * TOK, 128))
            weights.append(dec_v[origin])
        part = jnp.dot(
            jnp.concatenate(rows, axis=1),
            jnp.concatenate(weights, axis=0),
            preferred_element_type=F32,
        )
        pixels = part if pixels is None else pixels + part
    edges[0] = pixels[:TOK, :EDGE].astype(BF16)
    edges[1] = pixels[TOK:, -EDGE:].astype(BF16)

    to_near.start()
    tokens[1:3] = pixels.reshape(2, TQ, CG, ROWL * PATCH)

    lane = lax.broadcasted_iota(jnp.int32, (CG, CH), 1)

    def placed(slot, tq, start, place):
        base = min(start // 128 * 128, ROWL * PATCH - CH)
        block = tokens[slot, tq, :, base : base + CH]
        shift = (place - (start - base)) % CH
        return pltpu.roll(block, shift, 1) if shift else block

    def half(p, w):
        slot, pr, place = p // PATCH + 1, p % PATCH, p % 3 * 80
        tq, part = divmod(w, 4)
        if part:
            return placed(slot, tq, pr * ROWL + (part - 1) * 40, place)
        before = placed(slot, (tq - 1) % TQ, pr * ROWL + 120, place)
        own = placed(slot, tq % TQ, pr * ROWL, place + 40)
        if tq == 0:
            before = pltpu.roll(before, 1, 0)
        if tq == TQ:
            own = pltpu.roll(own, CG - 1, 0)
        return jnp.where(lane < place + 40, before, own)

    def spread(rows):
        for i in rows:
            values = [half(i - 3, w) for w in range(SIDES * PAIRS + 1)]
            for w in range(WIN):
                pieces[i, w] = jnp.concatenate([values[w], values[w + PAIRS]], axis=0).astype(BF16)

    lane2 = lax.broadcasted_iota(jnp.int32, (SUB, CH), 1)

    def first_rows(rows):
        for turn in range(3):
            mine = [j for j in rows if j % 3 == turn]
            windows = []
            for j in mine:
                parts = [pieces[j + (c - j) % 3] for c in range(3)]
                window = jnp.where(lane2 < 80, parts[0], jnp.where(lane2 < 160, parts[1], parts[2]))
                windows.append(window.reshape(WIN * SUB, CH))
            hidden = jnp.maximum(
                jnp.dot(
                    jnp.concatenate(windows, axis=0), in_v[turn], preferred_element_type=F32
                ),
                0.0,
            ).reshape(len(mine), WIN, SUB, 2 * CH)
            for at, j in enumerate(mine):
                left, right = hidden[at, :, :, :CH], hidden[at, :, :, CH:]
                if j < 2 or j >= FIRST - 2:
                    outside = top if j < 2 else bottom
                    left = jnp.where(outside, 0.0, left)
                    right = jnp.where(outside, 0.0, right)
                here = slice(j * STEP, (j + 1) * STEP)
                first[0, here] = (left[:-1] - left[1:]).reshape(STEP, CH).astype(BF16)
                first[1, here] = (right[:-1] + left[1:]).reshape(STEP, CH).astype(BF16)
                first[2, here] = (left[1:] - right[:-1]).reshape(STEP, CH).astype(BF16)
                first[3, here] = (right[:-1] - right[1:]).reshape(STEP, CH).astype(BF16)

    def second_rows(*spans):
        order = [i for low, high in spans for i in range(low, high)]
        count = len(order)
        products = []
        for k in range(4):
            blocks = []
            for a in range(3):
                parts = [first[k, (low + a) * STEP : (high + a) * STEP] for low, high in spans]
                blocks.append(jnp.concatenate(parts, axis=0))
            products.append(
                jnp.dot(jnp.concatenate(blocks, axis=1), mid_v[k], preferred_element_type=F32)
            )
        pair = (
            products[0] + (products[1] + products[2]),
            (products[1] - products[2]) - products[3],
        )
        pair = [jnp.maximum(x, 0.0).reshape(count, STEP, CH) for x in pair]
        rows = []
        for step, i in enumerate(order):
            values = [x[step] for x in pair]
            if i == 0:
                values = [jnp.where(top, 0.0, x) for x in values]
            if i == SECOND - 1:
                values = [jnp.where(bottom, 0.0, x) for x in values]
            rows += [x.astype(BF16) for x in values]
        return rows

    def last_taps(rows, slot):
        tap = lax.dot_general(
            out_v[...],
            jnp.concatenate(rows, axis=0),
            (((1,), (1,)), ((), ())),
            preferred_element_type=F32,
        )
        for i in range(len(rows) // 4):
            part = tap[:, i * 4 * STEP : (i + 1) * 4 * STEP]
            taps[slot + i] = jnp.concatenate([part[b * 8 : b * 8 + 8] for b in range(3)], axis=1)

    spread(range(3, 19))
    first_rows(range(3, 17))

    @pl.when(greets)
    def _():
        pl.semaphore_wait(ready, 1)
        to_far.start()

    last_taps(second_rows((3, 15)), 0)

    from_near.wait_recv()
    pl.when(greeted)(lambda: from_far.wait_recv())

    def decode(side, lanes):
        row = jnp.concatenate([beyond[k] for k in range(NLON)], axis=1)
        part = dec_v[:, :, lanes].reshape(NLON * 128, EDGE)
        halo[side] = jnp.dot(row, part, preferred_element_type=F32).astype(BF16)

    @pl.when(greets)
    def _():
        for step in FAR_FIRST:
            outward(step, False).wait_recv()
        pl.when(odd == 0)(lambda: decode(0, slice(ROWL * PATCH - EDGE, ROWL * PATCH)))
        pl.when(odd == 1)(lambda: decode(1, slice(0, EDGE)))

    tokens[0, :, :, -EDGE:] = halo[0].astype(F32).reshape(TQ, CG, EDGE)
    tokens[3, :, :, :EDGE] = halo[1].astype(F32).reshape(TQ, CG, EDGE)
    spread((0, 1, 2, 19, 20, 21))
    first_rows((0, 1, 2, 17, 18, 19))
    last_taps(second_rows((0, 3), (15, 18)), 6)

    for copy in last[NLON:]:
        copy.wait()
    for step in FAR_FIRST[:-1]:
        across(step, True).wait_send()
    to_near.wait_send()
    pl.when(greets)(lambda: to_far.wait_send())

    @pl.when(greeted)
    def _():
        for step in FAR_FIRST:
            outward(step, True).wait_send()


def order_kernel(taps, order_v, result, sums):
    count = taps.shape[0] * 8
    tap = taps[...].reshape(count, 3 * 4 * STEP)
    high = tap.astype(BF16)
    low = (tap - high.astype(F32)).astype(BF16)
    moved = jnp.dot(
        jnp.concatenate([high, low], axis=0), order_v[...], preferred_element_type=F32
    )
    sums[...] = moved[:count] + moved[count:]
    for p in range(ROWS):
        total = None
        for a in range(3):
            slot, half = divmod(SECOND_ORDER.index(p + a), 2)
            term = sums[slot * 8 + a : slot * 8 + a + 1, half * CH : half * CH + COLS]
            total = term if total is None else total + term
        result[p : p + 1, :] = total


def per_device(kept_modes, decoder_weight, conv_in_weight, conv_mid_weight, conv_out_weight):
    mode_count, chans = kept_modes.shape[1], kept_modes.shape[3]
    table = dft_table(mode_count)
    order = order_table()
    vmem = pl.BlockSpec(memory_space=pltpu.VMEM)
    dma = pltpu.SemaphoreType.DMA
    staged = pl.pallas_call(
        field_kernel,
        out_shape=(
            pltpu.VMEM((SECOND // 2, 8, 3 * 4 * STEP), F32),
            pltpu.VMEM(order.shape[1:], BF16),
        ),
        in_specs=[pl.BlockSpec(memory_space=pltpu.HBM)] * 7,
        out_specs=(vmem,) * 2,
        scratch_shapes=[
            pltpu.VMEM((2, NLON, TOK, 128), BF16),
            pltpu.VMEM((2, TOK, EDGE), BF16),
            pltpu.VMEM((2, TOK, EDGE), BF16),
            pltpu.VMEM((NLON, TOK, 128), BF16),
            pltpu.VMEM((NLON, 128, ROWL * PATCH), BF16),
            pltpu.VMEM((3, CH, 2 * CH), BF16),
            pltpu.VMEM((4, 3 * CH, CH), BF16),
            pltpu.VMEM((24, CH), BF16),
            pltpu.VMEM((4, TQ, CG, ROWL * PATCH), F32),
            pltpu.VMEM((PIX, WIN, SUB, CH), BF16),
            pltpu.VMEM((4, FIRST * STEP, CH), BF16),
            pltpu.VMEM(kept_modes.shape, BF16),
            pltpu.VMEM(table.shape, BF16),
            pltpu.VMEM((NLON, 2, TOK, 128), BF16),
            pltpu.VMEM(conv_in_weight.shape, BF16),
            pltpu.VMEM((3, CH, CH), BF16),
            pltpu.VMEM((3, 3, CH), BF16),
            pltpu.VMEM((24, CH), F32),
            dma((5,)),
            dma((NLON,)),
            dma((3, 3)),
            dma((2 * NLON + 2,)),
            dma((2 * NLON + 2,)),
            pltpu.SemaphoreType.REGULAR,
        ],
        compiler_params=pltpu.CompilerParams(
            collective_id=0, has_side_effects=True, vmem_limit_bytes=40 * 2**20
        ),
        name="field_to_taps",
    )(
        *[
            pltpu.with_memory_space_constraint(x, pltpu.HBM)
            for x in (
                kept_modes,
                jnp.asarray(table),
                jnp.asarray(order),
                decoder_weight,
                conv_in_weight,
                conv_mid_weight.reshape(9, CH, CH),
                conv_out_weight.reshape(3, 3, CH),
            )
        ]
    )
    staged = [pltpu.with_memory_space_constraint(x, pltpu.VMEM) for x in staged]
    return pl.pallas_call(
        order_kernel,
        out_shape=jax.ShapeDtypeStruct((ROWS, COLS), F32),
        in_specs=[vmem] * 2,
        out_specs=vmem,
        scratch_shapes=[pltpu.VMEM((SECOND // 2 * 8, 2 * CH), F32)],
        compiler_params=pltpu.CompilerParams(vmem_limit_bytes=16 * 2**20),
        name="order",
    )(*staged)


def solution(mesh):
    placed = (P("lat", None, None, "lon"), P(), P(), P(), P())
    return jax.shard_map(
        per_device, mesh=mesh, in_specs=placed, out_specs=P("lat", "lon"), check_vma=False
    )
```

```python
import math

import jax
import jax.numpy as jnp
import numpy as np
from jax import lax
from jax.experimental import pallas as pl
from jax.experimental.pallas import tpu as pltpu
from jax.sharding import PartitionSpec as P

MESH = pl.DeviceIdType.MESH
BF16 = jnp.bfloat16
F32 = jnp.float32

LON_TOK = 180
PATCH = 8
NLON = 8
COLS = 180
ROWS = 16
OUT = 20
FAR_FIRST = (2, 6, 1, 7, 3, 5, 4, 0)
CH = 256
TQ = 3
CG = 8
TOK = TQ * CG
SIDES = 2
T = TQ * PATCH // SIDES
SUB = SIDES * CG
WIN = (T + 2) // 2
PAIRS = T // 2
STEP = PAIRS * SUB
SECOND = ROWS + 2
FIRST = ROWS + 4
PIX = ROWS + 6
SECOND_ORDER = tuple(range(3, 15)) + (0, 1, 2, 15, 16, 17)
ROWL = PATCH * OUT
EDGE = 512


def first_token(sector):
    return (COLS * sector - 3) // PATCH


def dft_table(mode_count):
    ids = []
    for d in range(NLON):
        for tq in range(TQ):
            for cg in range(CG):
                ids.append((first_token(d) + cg * TQ + tq) % LON_TOK)
    modes = np.arange(mode_count)
    angle = (np.array(ids)[:, None] * modes[None, :] % LON_TOK) * (2.0 * math.pi / LON_TOK)
    scale = np.where(modes == 0, 1.0, 2.0) / math.sqrt(LON_TOK)
    table = np.stack([scale * np.cos(angle), -scale * np.sin(angle)], axis=2)
    table = table.reshape(len(ids), 2 * mode_count).astype(np.float32)
    high = table.astype(BF16)
    low = (table - high.astype(np.float32)).astype(BF16)
    return np.concatenate([high, low], axis=0)


def order_table():
    table = np.zeros((2, 3 * 4 * STEP, 2 * CH), np.float32)
    for parity in range(2):
        offset = COLS * parity - PATCH * first_token(parity)
        for b in range(3):
            for q in range(COLS):
                cg, rest = divmod(q + offset - 1 + b, T * SIDES)
                side, t = divmod(rest, T)
                pair, phase = divmod(t, 2)
                at = (b * 4 + phase) * STEP + pair * SUB + side * CG + cg
                for row in range(2):
                    table[parity, at + row * 2 * STEP, row * CH + q] = 1.0
    return table.astype(BF16)


def field_kernel(
    modes_ref, table_ref, order_ref, dec_ref, in_ref, mid_ref, out_ref,
    taps, order_v,
    field, edges, halo, beyond, dec_v, in_v, mid_v, out_v, tokens, pieces, first,
    modes_s, table_s, send, in_s, mid_s, out_s, out_f,
    local_sem, dec_sem, mid_sem, send_sem, recv_sem, ready,
):
    lat, lon = lax.axis_index("lat"), lax.axis_index("lon")
    nlat = lax.axis_size("lat")
    chans = modes_s.shape[3]
    mode_count = modes_s.shape[1]

    early = [
        pltpu.make_async_copy(modes_ref, modes_s, local_sem.at[0]),
        pltpu.make_async_copy(table_ref, table_s, local_sem.at[1]),
    ]
    late = [
        pltpu.make_async_copy(in_ref, in_s, local_sem.at[2]),
        pltpu.make_async_copy(out_ref, out_s, local_sem.at[3]),
    ]
    middle = [
        pltpu.make_async_copy(
            mid_ref.at[a * 3 + b],
            mid_s.at[a] if b == 1 else mid_v.at[3 * b // 2, a * CH : (a + 1) * CH],
            mid_sem.at[a, b],
        )
        for a in range(3)
        for b in range(3)
    ]
    last = [
        pltpu.make_async_copy(
            dec_ref.at[k * chans : (k + 1) * chans], dec_v.at[k, 0:chans], dec_sem.at[k]
        )
        for k in range(NLON)
    ] + [
        pltpu.make_async_copy(order_ref.at[lax.rem(lon, 2)], order_v, local_sem.at[4]),
    ]
    for copy in early:
        copy.start()
    barrier = pltpu.get_barrier_semaphore()

    odd = lax.rem(lat, 2)
    near = lat + 1 - 2 * odd
    far = lat - 1 + 2 * odd
    has_far = (far >= 0) & (far < nlat)

    upper = jnp.minimum(lat, far)
    swap = (lax.rem(upper, 4) == 3) & (upper >= nlat // 2)
    leads = (odd == 1) != swap
    greets, greeted = has_far & leads, has_far & jnp.logical_not(leads)

    def greet(semaphore, row, column):
        there = {"lat": row, "lon": column}
        pl.semaphore_signal(semaphore, inc=1, device_id=there, device_id_type=MESH)

    for step in FAR_FIRST[:-1]:
        greet(barrier, lat, lax.rem(lon + step, NLON))

    @pl.when(greets)
    def _():
        for step in FAR_FIRST:
            greet(barrier, far, lax.rem(lon + step, NLON))

    greet(barrier, near, lon)
    for copy in late + middle + last:
        copy.start()
    send[...] = jnp.zeros_like(send)
    for copy in early:
        copy.wait()
    for row in range(2):
        values = modes_s[row].reshape(2 * mode_count, chans)
        wide = jnp.dot(table_s[...], values, preferred_element_type=F32)
        half = wide.shape[0] // 2
        whole = (wide[:half] + wide[half:]).astype(BF16)
        send[:, row, :, 0:chans] = whole.reshape(NLON, TOK, chans)
    for row in range(2):
        field[row, lon] = send[lon, row]
    pl.semaphore_wait(barrier, NLON + NLON * greeted.astype(jnp.int32))
    pl.when(greeted)(lambda: greet(ready, far, lon))

    def across(step, mine):
        there = lax.rem(lon + step, NLON)
        owner = lon if mine else lax.rem(lon + NLON - step, NLON)
        return pltpu.make_async_remote_copy(
            src_ref=send.at[there],
            dst_ref=field.at[:, owner],
            send_sem=send_sem.at[step],
            recv_sem=recv_sem.at[step],
            device_id={"lat": lat, "lon": there},
            device_id_type=MESH,
        )

    def outward(step, mine):
        owner = lon if mine else lax.rem(lon + NLON - step, NLON)
        there = lax.rem(lon + step, NLON)
        return pltpu.make_async_remote_copy(
            src_ref=send.at[there, odd],
            dst_ref=beyond.at[owner],
            send_sem=send_sem.at[NLON + 2 + step],
            recv_sem=recv_sem.at[NLON + 2 + step],
            device_id={"lat": far, "lon": there},
            device_id_type=MESH,
        )

    def onward(way, row, source, target):
        return pltpu.make_async_remote_copy(
            src_ref=edges.at[source],
            dst_ref=halo.at[target],
            send_sem=send_sem.at[NLON + way],
            recv_sem=recv_sem.at[NLON + way],
            device_id={"lat": row, "lon": lon},
            device_id_type=MESH,
        )

    to_near, from_near = (onward(0, near, 1 - odd, slot) for slot in (odd, 1 - odd))
    to_far, from_far = (onward(1, far, odd, slot) for slot in (1 - odd, odd))

    for step in FAR_FIRST[:-1]:
        across(step, True).start()

    @pl.when(greeted)
    def _():
        for step in FAR_FIRST:
            outward(step, True).start()

    @pl.when(jnp.logical_not(has_far))
    def _():
        halo[odd] = jnp.zeros(halo.shape[1:], BF16)

    for copy in late:
        copy.wait()
    dec_v[:, chans:, :] = jnp.zeros((NLON, dec_v.shape[1] - chans, dec_v.shape[2]), BF16)
    for turn in range(3):
        for phase in range(2):
            rows = []
            for place in range(3):
                a = (place - turn) % 3
                if phase:
                    rows.append(jnp.zeros((OUT, CH), BF16))
                rows += [in_s[a, b] for b in range(3)]
                if not phase:
                    rows.append(jnp.zeros((OUT, CH), BF16))
            rows.append(jnp.zeros((16, CH), BF16))
            in_v[turn, :, phase * CH : (phase + 1) * CH] = jnp.concatenate(rows, axis=0)
    out_f[...] = jnp.zeros_like(out_f)
    for a in range(3):
        for b in range(3):
            out_f[b * 8 + a : b * 8 + a + 1, :] = out_s[a, b : b + 1, :].astype(F32)
    out_v[...] = out_f[...].astype(BF16)
    for copy in middle:
        copy.wait()
    for a in range(3):
        here = slice(a * CH, (a + 1) * CH)
        ends = mid_v[0, here].astype(F32) + mid_v[3, here].astype(F32)
        centre = mid_s[a].astype(F32)
        mid_v[1, here] = (0.5 * (ends + centre)).astype(BF16)
        mid_v[2, here] = (0.5 * (ends - centre)).astype(BF16)
    for copy in last[:NLON]:
        copy.wait()
    top, bottom = lat == 0, lat == nlat - 1
    pixels = None
    for group in ((0, 4), (3, 5), (1, 7), (2, 6)):
        rows, weights = [], []
        for step in group:
            if step:
                across(step, False).wait_recv()
            origin = lax.rem(lon + NLON - step, NLON)
            rows.append(field[:, origin].reshape(2 * TOK, 128))
            weights.append(dec_v[origin])
        part = jnp.dot(
            jnp.concatenate(rows, axis=1),
            jnp.concatenate(weights, axis=0),
            preferred_element_type=F32,
        )
        pixels = part if pixels is None else pixels + part
    edges[0] = pixels[:TOK, :EDGE].astype(BF16)
    edges[1] = pixels[TOK:, -EDGE:].astype(BF16)

    to_near.start()
    tokens[1:3] = pixels.reshape(2, TQ, CG, ROWL * PATCH)

    lane = lax.broadcasted_iota(jnp.int32, (CG, CH), 1)

    def placed(slot, tq, start, place):
        base = min(start // 128 * 128, ROWL * PATCH - CH)
        block = tokens[slot, tq, :, base : base + CH]
        shift = (place - (start - base)) % CH
        return pltpu.roll(block, shift, 1) if shift else block

    def half(p, w):
        slot, pr, place = p // PATCH + 1, p % PATCH, p % 3 * 80
        tq, part = divmod(w, 4)
        if part:
            return placed(slot, tq, pr * ROWL + (part - 1) * 40, place)
        before = placed(slot, (tq - 1) % TQ, pr * ROWL + 120, place)
        own = placed(slot, tq % TQ, pr * ROWL, place + 40)
        if tq == 0:
            before = pltpu.roll(before, 1, 0)
        if tq == TQ:
            own = pltpu.roll(own, CG - 1, 0)
        return jnp.where(lane < place + 40, before, own)

    def spread(rows):
        for i in rows:
            values = [half(i - 3, w) for w in range(SIDES * PAIRS + 1)]
            for w in range(WIN):
                pieces[i, w] = jnp.concatenate([values[w], values[w + PAIRS]], axis=0).astype(BF16)

    lane2 = lax.broadcasted_iota(jnp.int32, (SUB, CH), 1)

    def first_rows(rows):
        for turn in range(3):
            mine = [j for j in rows if j % 3 == turn]
            windows = []
            for j in mine:
                parts = [pieces[j + (c - j) % 3] for c in range(3)]
                window = jnp.where(lane2 < 80, parts[0], jnp.where(lane2 < 160, parts[1], parts[2]))
                windows.append(window.reshape(WIN * SUB, CH))
            hidden = jnp.maximum(
                jnp.dot(
                    jnp.concatenate(windows, axis=0), in_v[turn], preferred_element_type=F32
                ),
                0.0,
            ).reshape(len(mine), WIN, SUB, 2 * CH)
            for at, j in enumerate(mine):
                left, right = hidden[at, :, :, :CH], hidden[at, :, :, CH:]
                if j < 2 or j >= FIRST - 2:
                    outside = top if j < 2 else bottom
                    left = jnp.where(outside, 0.0, left)
                    right = jnp.where(outside, 0.0, right)
                here = slice(j * STEP, (j + 1) * STEP)
                first[0, here] = (left[:-1] - left[1:]).reshape(STEP, CH).astype(BF16)
                first[1, here] = (right[:-1] + left[1:]).reshape(STEP, CH).astype(BF16)
                first[2, here] = (left[1:] - right[:-1]).reshape(STEP, CH).astype(BF16)
                first[3, here] = (right[:-1] - right[1:]).reshape(STEP, CH).astype(BF16)

    def second_rows(*spans):
        order = [i for low, high in spans for i in range(low, high)]
        count = len(order)
        products = []
        for k in range(4):
            blocks = []
            for a in range(3):
                parts = [first[k, (low + a) * STEP : (high + a) * STEP] for low, high in spans]
                blocks.append(jnp.concatenate(parts, axis=0))
            products.append(
                jnp.dot(jnp.concatenate(blocks, axis=1), mid_v[k], preferred_element_type=F32)
            )
        pair = (
            products[0] + (products[1] + products[2]),
            (products[1] - products[2]) - products[3],
        )
        pair = [jnp.maximum(x, 0.0).reshape(count, STEP, CH) for x in pair]
        rows = []
        for step, i in enumerate(order):
            values = [x[step] for x in pair]
            if i == 0:
                values = [jnp.where(top, 0.0, x) for x in values]
            if i == SECOND - 1:
                values = [jnp.where(bottom, 0.0, x) for x in values]
            rows += [x.astype(BF16) for x in values]
        return rows

    def last_taps(rows, slot):
        tap = lax.dot_general(
            out_v[...],
            jnp.concatenate(rows, axis=0),
            (((1,), (1,)), ((), ())),
            preferred_element_type=F32,
        )
        for i in range(len(rows) // 4):
            part = tap[:, i * 4 * STEP : (i + 1) * 4 * STEP]
            taps[slot + i] = jnp.concatenate([part[b * 8 : b * 8 + 8] for b in range(3)], axis=1)

    spread(range(3, 19))
    first_rows(range(3, 17))

    @pl.when(greets)
    def _():
        pl.semaphore_wait(ready, 1)
        to_far.start()

    last_taps(second_rows((3, 15)), 0)

    from_near.wait_recv()
    pl.when(greeted)(lambda: from_far.wait_recv())

    def decode(side, lanes):
        row = jnp.concatenate([beyond[k] for k in range(NLON)], axis=1)
        part = dec_v[:, :, lanes].reshape(NLON * 128, EDGE)
        halo[side] = jnp.dot(row, part, preferred_element_type=F32).astype(BF16)

    @pl.when(greets)
    def _():
        for step in FAR_FIRST:
            outward(step, False).wait_recv()
        pl.when(odd == 0)(lambda: decode(0, slice(ROWL * PATCH - EDGE, ROWL * PATCH)))
        pl.when(odd == 1)(lambda: decode(1, slice(0, EDGE)))

    tokens[0, :, :, -EDGE:] = halo[0].astype(F32).reshape(TQ, CG, EDGE)
    tokens[3, :, :, :EDGE] = halo[1].astype(F32).reshape(TQ, CG, EDGE)
    spread((0, 1, 2, 19, 20, 21))
    first_rows((0, 1, 2, 17, 18, 19))
    last_taps(second_rows((0, 3), (15, 18)), 6)

    for copy in last[NLON:]:
        copy.wait()
    for step in FAR_FIRST[:-1]:
        across(step, True).wait_send()
    to_near.wait_send()
    pl.when(greets)(lambda: to_far.wait_send())

    @pl.when(greeted)
    def _():
        for step in FAR_FIRST:
            outward(step, True).wait_send()


def order_kernel(taps, order_v, result, sums):
    count = taps.shape[0] * 8
    tap = taps[...].reshape(count, 3 * 4 * STEP)
    high = tap.astype(BF16)
    low = (tap - high.astype(F32)).astype(BF16)
    moved = jnp.dot(
        jnp.concatenate([high, low], axis=0), order_v[...], preferred_element_type=F32
    )
    sums[...] = moved[:count] + moved[count:]
    for p in range(ROWS):
        total = None
        for a in range(3):
            slot, half = divmod(SECOND_ORDER.index(p + a), 2)
            term = sums[slot * 8 + a : slot * 8 + a + 1, half * CH : half * CH + COLS]
            total = term if total is None else total + term
        result[p : p + 1, :] = total


def per_device(kept_modes, decoder_weight, conv_in_weight, conv_mid_weight, conv_out_weight):
    mode_count, chans = kept_modes.shape[1], kept_modes.shape[3]
    table = dft_table(mode_count)
    order = order_table()
    vmem = pl.BlockSpec(memory_space=pltpu.VMEM)
    dma = pltpu.SemaphoreType.DMA
    staged = pl.pallas_call(
        field_kernel,
        out_shape=(
            pltpu.VMEM((SECOND // 2, 8, 3 * 4 * STEP), F32),
            pltpu.VMEM(order.shape[1:], BF16),
        ),
        in_specs=[pl.BlockSpec(memory_space=pltpu.HBM)] * 7,
        out_specs=(vmem,) * 2,
        scratch_shapes=[
            pltpu.VMEM((2, NLON, TOK, 128), BF16),
            pltpu.VMEM((2, TOK, EDGE), BF16),
            pltpu.VMEM((2, TOK, EDGE), BF16),
            pltpu.VMEM((NLON, TOK, 128), BF16),
            pltpu.VMEM((NLON, 128, ROWL * PATCH), BF16),
            pltpu.VMEM((3, CH, 2 * CH), BF16),
            pltpu.VMEM((4, 3 * CH, CH), BF16),
            pltpu.VMEM((24, CH), BF16),
            pltpu.VMEM((4, TQ, CG, ROWL * PATCH), F32),
            pltpu.VMEM((PIX, WIN, SUB, CH), BF16),
            pltpu.VMEM((4, FIRST * STEP, CH), BF16),
            pltpu.VMEM(kept_modes.shape, BF16),
            pltpu.VMEM(table.shape, BF16),
            pltpu.VMEM((NLON, 2, TOK, 128), BF16),
            pltpu.VMEM(conv_in_weight.shape, BF16),
            pltpu.VMEM((3, CH, CH), BF16),
            pltpu.VMEM((3, 3, CH), BF16),
            pltpu.VMEM((24, CH), F32),
            dma((5,)),
            dma((NLON,)),
            dma((3, 3)),
            dma((2 * NLON + 2,)),
            dma((2 * NLON + 2,)),
            pltpu.SemaphoreType.REGULAR,
        ],
        compiler_params=pltpu.CompilerParams(
            collective_id=0, has_side_effects=True, vmem_limit_bytes=40 * 2**20
        ),
        name="field_to_taps",
    )(
        *[
            pltpu.with_memory_space_constraint(x, pltpu.HBM)
            for x in (
                kept_modes,
                jnp.asarray(table),
                jnp.asarray(order),
                decoder_weight,
                conv_in_weight,
                conv_mid_weight.reshape(9, CH, CH),
                conv_out_weight.reshape(3, 3, CH),
            )
        ]
    )
    staged = [pltpu.with_memory_space_constraint(x, pltpu.VMEM) for x in staged]
    return pl.pallas_call(
        order_kernel,
        out_shape=jax.ShapeDtypeStruct((ROWS, COLS), F32),
        in_specs=[vmem] * 2,
        out_specs=vmem,
        scratch_shapes=[pltpu.VMEM((SECOND // 2 * 8, 2 * CH), F32)],
        compiler_params=pltpu.CompilerParams(vmem_limit_bytes=16 * 2**20),
        name="order",
    )(*staged)


def solution(mesh):
    placed = (P("lat", None, None, "lon"), P(), P(), P(), P())
    return jax.shard_map(
        per_device, mesh=mesh, in_specs=placed, out_specs=P("lat", "lon"), check_vma=False
    )
```
